256 devices in a mesh: row: 32 (over z_lo, y, x), col: 8 (over z_hi, core).
Axes of the slice: x: 4, y: 4, z: 8 (z_hi: 4, z_lo: 2; z = z_hi * 2 + z_lo), core: 2. Of those that a mesh axis runs over, the one named last changes fastest.
Arguments:
- features: bfloat16 [512, 512, 1024], P('row', None, 'col'), may hold values from -6 to 6
- projection: bfloat16 [512, 4], replicated, may hold values from -0.25 to 0.25
- norm_gain: bfloat16 [2048], replicated, may hold values from 0.25 to 1.75
- norm_shift: bfloat16 [2048], replicated, may hold values from -6 to 6
- weight_in: bfloat16 [2048, 4096], P(None, 'col'), may hold values from -0.125 to 0.125
- weight_out: bfloat16 [4096, 1, 1024], P('col'), may hold values from -0.09375 to 0.09375
- cotangent: bfloat16 [512, 1, 1024], P('row', None, 'col'), may hold values from -6 to 6
Outputs:
- mixed: bfloat16 [512, 1, 1024], P('row', None, 'col')
- grad_features: bfloat16 [512, 512, 1024], P('row', None, 'col')
- grad_gain: float32 [2048], replicated
- grad_shift: float32 [2048], replicated
- grad_weight_in: bfloat16 [2048, 4096], P(None, 'col')
- grad_weight_out: bfloat16 [4096, 1, 1024], P('col')
The draws below stay inside these ranges and needn't reach their ends.
All inputs are finite; a program needn't handle non-finite values.
Results may differ from the reference program's by a relative error of at most 0.013.
Values may be sent and summed in bfloat16 or wider, within the bound.
A program may use at most 64 MiB of HBM per device.

```python
import jax
import jax.numpy as jnp
from jax import lax

N = 512
D = 1024
K = 4
H = 4096
NF = 1
ROWS = 512


def block_scale(key, extent, cuts, smallest, top_value):
    gain = 1.0
    for dim, shards_of in cuts:
        draws = jax.random.uniform(jax.random.fold_in(jax.random.fold_in(key, 6), dim), (shards_of,), jnp.float32, smallest / len(cuts), top_value / len(cuts))
        gain = gain * jnp.repeat(jnp.exp(draws), extent[dim] // shards_of).reshape((-1,) + (1,) * (len(extent) - 1 - dim))
    return gain


def bell_draw(stream_key, shape, deviation, bound, pieces=(), dtype=jnp.bfloat16):
    result = jax.random.normal(stream_key, shape, jnp.float32) * deviation
    if len(pieces) > 0:
        result = block_scale(stream_key, shape, pieces, -0.22, 0.18) * result
    return jnp.clip(result, min=-bound, max=bound).astype(dtype)


def setup_inputs(seed: int = 0) -> dict:
    keys = jax.random.split(jax.random.key(seed), 8)
    features = bell_draw(keys[0], (ROWS, N, D), 1.0, 6.0, ((0, 32), (2, 8)))
    projection = bell_draw(keys[1], (N, K), N ** -0.5, 0.25)
    norm_gain = jnp.clip(1.0 + 0.15 * jax.random.normal(keys[2], (N * K,), jnp.float32), 0.25, 1.75).astype(jnp.bfloat16)
    norm_shift = bell_draw(keys[3], (N * K,), 1.0, 6.0)
    weight_in = bell_draw(keys[4], (N * K, H), (N * K) ** -0.5, 0.125, ((1, 8),))
    weight_out = bell_draw(keys[5], (H, NF, D), H ** -0.5, 0.09375, ((0, 8),))
    cotangent = bell_draw(keys[6], (ROWS, NF, D), 1.0, 6.0, ((0, 32), (2, 8)))
    return dict(features=features, projection=projection, norm_gain=norm_gain, norm_shift=norm_shift, weight_in=weight_in, weight_out=weight_out, cotangent=cotangent)


def layer_norm(inter, norm_gain, norm_shift):
    mean = lax.optimization_barrier(jnp.mean(inter, axis=1, keepdims=True))
    centered = inter - mean
    rstd = lax.rsqrt(lax.optimization_barrier(jnp.mean(centered * centered, axis=1, keepdims=True)) + 1e-05)
    unit = centered * rstd
    normed = (unit * norm_gain.astype(jnp.float32) + norm_shift.astype(jnp.float32)).astype(jnp.bfloat16)
    return (normed, unit, rstd)

def reference(features, projection, norm_gain, norm_shift, weight_in, weight_out, cotangent):
    batch = features.shape[0]
    hidden = weight_in.shape[1]
    feats = features.astype(jnp.float32)
    proj = projection.astype(jnp.float32)
    reduced = jnp.einsum('bnd,nk->bdk', feats, proj).astype(jnp.bfloat16)
    inter = jnp.einsum('bnd,bdk->bnk', feats, reduced.astype(jnp.float32)).reshape(batch, -1)
    normed, unit, rstd = layer_norm(inter, norm_gain, norm_shift)
    pre = jnp.dot(normed, weight_in, preferred_element_type=jnp.float32)
    act = jax.nn.silu(pre).astype(jnp.bfloat16)
    wide_out = weight_out.reshape(hidden, -1)
    mixed = jnp.dot(act, wide_out, preferred_element_type=jnp.float32).astype(jnp.bfloat16).reshape(cotangent.shape)
    grads = cotangent.reshape(batch, -1)
    dact = jnp.dot(grads, wide_out.T, preferred_element_type=jnp.float32)
    sigma = jax.nn.sigmoid(pre)
    dpre = (dact * sigma * (1.0 + pre * (1.0 - sigma))).astype(jnp.bfloat16)
    grad_weight_out = jnp.dot(act.T, grads, preferred_element_type=jnp.float32).astype(jnp.bfloat16).reshape(weight_out.shape)
    grad_weight_in = jnp.dot(normed.T, dpre, preferred_element_type=jnp.float32).astype(jnp.bfloat16)
    dnormed = jnp.dot(dpre, weight_in.T, preferred_element_type=jnp.float32)
    grad_gain = lax.optimization_barrier(jnp.sum(dnormed * unit, axis=0))
    grad_shift = lax.optimization_barrier(jnp.sum(dnormed, axis=0))
    scaled = dnormed * norm_gain.astype(jnp.float32)
    dinter = rstd * (scaled - lax.optimization_barrier(jnp.mean(scaled, axis=1, keepdims=True)) - unit * lax.optimization_barrier(jnp.mean(scaled * unit, axis=1, keepdims=True)))
    dinter = dinter.reshape(batch, features.shape[1], -1)
    dreduced = jnp.einsum('bnd,bnk->bdk', feats, dinter)
    grad_features = jnp.einsum('bnk,bdk->bnd', dinter, reduced.astype(jnp.float32))
    grad_features = grad_features + jnp.einsum('nk,bdk->bnd', proj, dreduced)
    return (mixed, grad_features.astype(jnp.bfloat16), grad_gain, grad_shift, grad_weight_in, grad_weight_out)
```

```python
import functools

import jax
import jax.numpy as jnp
from jax import lax
from jax.experimental import pallas as pl
from jax.experimental.pallas import tpu as pltpu
from jax.sharding import PartitionSpec as P

MESH = pl.DeviceIdType.MESH
F32 = jnp.float32
BF16 = jnp.bfloat16
NT = (((1,), (1,)), ((), ()))


class Links:
    def __init__(self, send_sems, recv_sems):
        self.send_sems = send_sems
        self.recv_sems = recv_sems
        self.count = 0
        self.sends = []

    def start(self, src, dst, land, row, col):
        i = self.count
        self.count += 1
        copy = pltpu.make_async_remote_copy(
            src_ref=src,
            dst_ref=dst,
            send_sem=self.send_sems.at[i],
            recv_sem=self.recv_sems.at[i],
            device_id={"row": row, "col": col},
            device_id_type=MESH,
        )
        copy.start()
        self.sends.append(copy)
        return pltpu.make_async_remote_copy(
            src_ref=land,
            dst_ref=land,
            send_sem=self.send_sems.at[i],
            recv_sem=self.recv_sems.at[i],
            device_id={"row": row, "col": col},
            device_id_type=MESH,
        )


class Gather:
    def __init__(self, links, buf, where):
        self.links = links
        self.buf = buf
        self.x, self.y, self.zl, self.core, self.row, self.col = where
        core = self.core
        self.f = (1 - core) * self.x + core * self.y
        self.s = (1 - core) * self.y + core * self.x
        self.first = {}
        self.second = {}
        self.relay_first = []
        self.relay_second = {}
        self.sibling = []

    def pos(self, core, df, ds):
        f = (1 - core) * self.x + core * self.y
        s = (1 - core) * self.y + core * self.x
        f = lax.rem(f + df + 4, 4)
        s = lax.rem(s + ds + 4, 4)
        return (1 - core) * (s * 4 + f) + core * (f * 4 + s)

    def block(self, df, ds, zl=None, core=None):
        core = self.core if core is None else core
        p = self.pos(core, df, ds) * 32
        if zl is None:
            return self.buf.at[core, pl.ds(pl.multiple_of(p, 32), 32), :]
        return self.buf.at[core, pl.ds(pl.multiple_of(p + zl * 16, 16), 16), :]

    def row_of(self, df, ds):
        return self.zl * 16 + self.pos(self.core, df, ds)

    def start_z(self):
        mine = self.block(0, 0, self.zl)
        mate = (1 - self.zl) * 16 + self.pos(self.core, 0, 0)
        self.z = self.links.start(mine, mine, self.block(0, 0, 1 - self.zl), mate, self.col)

    def to_sibling(self, df, ds, zl=None):
        mine = self.block(df, ds, zl)
        other = 1 - self.core
        self.sibling.append(
            self.links.start(
                mine, mine, self.block(df, ds, zl, core=other), self.row, self.col + 1 - 2 * self.core
            )
        )

    def start_first(self):
        self.z.wait_recv()
        mine = self.block(0, 0)
        for d in (1, -1):
            self.first[d] = self.links.start(mine, mine, self.block(-d, 0), self.row_of(d, 0), self.col)
        self.start_second(0)
        self.to_sibling(0, 0, 1 - self.zl)

    def start_second(self, df):
        mine = self.block(df, 0)
        for d in (1, -1):
            self.second[df, d] = self.links.start(
                mine, mine, self.block(df, -d), self.row_of(0, d), self.col
            )

    def relay_firsts(self):
        for d in (1, -1):
            zl = (1 - d) // 2
            self.first[d].wait_recv()
            part = self.block(-d, 0, zl)
            self.relay_first.append(
                self.links.start(part, part, self.block(2, 0, zl), self.row_of(d, 0), self.col)
            )
        for d in (1, -1):
            self.start_second(-d)
        for d in (1, -1):
            self.to_sibling(-d, 0)

    def end_first(self):
        for copy in self.relay_first:
            copy.wait_recv()
        self.start_second(2)
        self.to_sibling(2, 0)

    def relay_seconds(self, df):
        self.relay_second[df] = []
        for d in (1, -1):
            zl = (1 - d) // 2
            self.second[df, d].wait_recv()
            part = self.block(df, -d, zl)
            self.relay_second[df].append(
                self.links.start(part, part, self.block(df, 2, zl), self.row_of(0, d), self.col)
            )
        for d in (1, -1):
            self.to_sibling(df, -d)

    def end_second(self, df):
        for copy in self.relay_second[df]:
            copy.wait_recv()
        self.to_sibling(df, 2)

    def end(self):
        for copy in self.sibling:
            copy.wait_recv()


def exchange(
    part_ref, cot_ref, gain_ref, shift_ref, win_ref, wout_ref,
    dinter_ref, mixed_ref, terms_ref, rows_ref, cots_ref,
    sums_ref, inter_ref, unit_ref, pieces_ref, got_ref, out_ref, got_out_ref, full_ref,
    sum_x_ref, sum_y_ref, sum_z_ref, sum_all_ref,
    send_sems, recv_sems, local_sem,
):
    row = lax.axis_index("row")
    col = lax.axis_index("col")
    x = lax.rem(row, 4)
    y = lax.rem(row // 4, 4)
    zl = row // 16
    core = lax.rem(col, 2)
    peers = [lax.rem(col + k, 8) for k in range(1, 8)]
    sources = [lax.rem(col + 8 - k, 8) for k in range(1, 8)]
    xs = [zl * 16 + y * 4 + lax.rem(x + k, 4) for k in range(1, 4)]
    ys = [zl * 16 + lax.rem(y + k, 4) * 4 + x for k in range(1, 4)]
    mate = (1 - zl) * 16 + y * 4 + x

    barrier = pltpu.get_barrier_semaphore()
    for peer in peers:
        pl.semaphore_signal(barrier, inc=1, device_id={"row": row, "col": peer}, device_id_type=MESH)
    for other in xs + ys + [mate]:
        pl.semaphore_signal(barrier, inc=1, device_id={"row": other, "col": col}, device_id_type=MESH)
    pl.semaphore_wait(barrier, 14)

    links = Links(send_sems, recv_sems)
    where = (x, y, zl, core, row, col)
    gather_n = Gather(links, rows_ref, where)
    gather_c = Gather(links, cots_ref, where)
    here = pl.ds(pl.multiple_of((y * 4 + x) * 32 + zl * 16, 16), 16)

    inters = [
        links.start(part_ref.at[peer], sums_ref.at[k], sums_ref.at[k], row, peer)
        for k, peer in enumerate(peers)
    ]

    def cot_place(c):
        return cots_ref.at[c // 4, here, pl.ds(pl.multiple_of(lax.rem(c, 4) * 128, 128), 128)]

    own = pltpu.make_async_copy(cot_ref, cot_place(col), local_sem)
    own.start()
    slices = [
        links.start(cot_ref, cot_place(col), cot_place(source), row, peer)
        for peer, source in zip(peers, sources)
    ]
    total = part_ref[col]
    for k, copy in enumerate(inters):
        copy.wait_recv()
        total = total + sums_ref[k]
    inter_ref[col] = total
    inters = [
        links.start(inter_ref.at[col], inter_ref.at[col], inter_ref.at[source], row, peer)
        for peer, source in zip(peers, sources)
    ]
    own.wait()
    for copy in slices:
        copy.wait_recv()
    gather_c.start_z()
    dact = jnp.zeros((16, 512), F32)
    for half in range(2):
        dact = dact + lax.dot_general(
            cots_ref[half, here, :],
            wout_ref[:, half * 512 : (half + 1) * 512],
            NT,
            preferred_element_type=F32,
        )
    for copy in inters:
        copy.wait_recv()

    total = inter_ref[0]
    for j in range(1, 8):
        total = total + inter_ref[j]
    mean = jnp.sum(total, axis=1, keepdims=True) * (1.0 / 2048)
    square = jnp.zeros((16, 256), F32)
    for j in range(8):
        centered = inter_ref[j] - mean
        square = square + centered * centered
    rstd = lax.rsqrt(jnp.sum(square, axis=1, keepdims=True) * (1.0 / 2048) + 1e-05)
    pre = jnp.zeros((16, 512), F32)
    normed = []
    for j in range(8):
        at = slice(j * 256, (j + 1) * 256)
        unit = (inter_ref[j] - mean) * rstd
        unit_ref[j] = unit
        normed.append(
            (unit * gain_ref[:, at].astype(F32) + shift_ref[:, at].astype(F32)).astype(BF16)
        )
        rows_ref[j // 4, here, (j % 4) * 256 : (j % 4 + 1) * 256] = normed[j]
    gather_n.start_z()
    gather_c.start_first()
    for j in range(8):
        at = slice(j * 256, (j + 1) * 256)
        pre = pre + jnp.dot(normed[j], win_ref[at, :], preferred_element_type=F32)
    sigma = 1.0 / (1.0 + jnp.exp(-pre))
    act = (pre * sigma).astype(BF16)
    dpre = (dact * sigma * (1.0 + pre * (1.0 - sigma))).astype(BF16)
    for j in range(8):
        at = slice(j * 256, (j + 1) * 256)
        pieces_ref[j] = lax.dot_general(dpre, win_ref[at, :], NT, preferred_element_type=F32)
    dnormeds = [
        links.start(pieces_ref.at[peer], got_ref.at[k], got_ref.at[k], row, peer)
        for k, peer in enumerate(peers)
    ]
    gather_n.start_first()
    for j in range(8):
        out_ref[j] = jnp.dot(
            act, wout_ref[:, j * 128 : (j + 1) * 128], preferred_element_type=F32
        )
    outs = [
        links.start(out_ref.at[peer], got_out_ref.at[k], got_out_ref.at[k], row, peer)
        for k, peer in enumerate(peers)
    ]
    gather_c.relay_firsts()

    dnormed = pieces_ref[col]
    for k, copy in enumerate(dnormeds):
        copy.wait_recv()
        dnormed = dnormed + got_ref[k]
    full_ref[col] = dnormed
    dnormeds = [
        links.start(full_ref.at[col], full_ref.at[col], full_ref.at[source], row, peer)
        for peer, source in zip(peers, sources)
    ]
    gain_terms = jnp.sum(dnormed * unit_ref[col], axis=0, keepdims=True)
    shift_terms = jnp.sum(dnormed, axis=0, keepdims=True)
    sum_x_ref[x] = jnp.concatenate([gain_terms, shift_terms, jnp.zeros((6, 256), F32)], axis=0)
    sums = [
        links.start(sum_x_ref.at[x], sum_x_ref.at[x], sum_x_ref.at[lax.rem(x + 4 - k, 4)], xs[k - 1], col)
        for k in range(1, 4)
    ]
    gather_n.relay_firsts()
    gather_c.end_first()

    for copy in dnormeds:
        copy.wait_recv()
    first = jnp.zeros((16, 256), F32)
    second = jnp.zeros((16, 256), F32)
    for j in range(8):
        at = slice(j * 256, (j + 1) * 256)
        scaled = full_ref[j] * gain_ref[:, at].astype(F32)
        first = first + scaled
        second = second + scaled * unit_ref[j]
    first = jnp.sum(first, axis=1, keepdims=True) * (1.0 / 2048)
    second = jnp.sum(second, axis=1, keepdims=True) * (1.0 / 2048)
    for j in range(8):
        at = slice(j * 256, (j + 1) * 256)
        scaled = full_ref[j] * gain_ref[:, at].astype(F32)
        dinter_ref[:, at] = rstd * (scaled - first - unit_ref[j] * second)

    gather_n.end_first()
    for copy in sums:
        copy.wait_recv()
    sum_y_ref[y] = (sum_x_ref[0] + sum_x_ref[1]) + (sum_x_ref[2] + sum_x_ref[3])
    sums = [
        links.start(sum_y_ref.at[y], sum_y_ref.at[y], sum_y_ref.at[lax.rem(y + 4 - k, 4)], ys[k - 1], col)
        for k in range(1, 4)
    ]
    mixed = out_ref[col]
    for k, copy in enumerate(outs):
        copy.wait_recv()
        mixed = mixed + got_out_ref[k]
    mixed_ref[...] = mixed.astype(BF16)

    order = (0, -1, 1, 2)
    for df in order:
        gather_c.relay_seconds(df)
    for copy in sums:
        copy.wait_recv()
    sum_z_ref[zl] = (sum_y_ref[0] + sum_y_ref[1]) + (sum_y_ref[2] + sum_y_ref[3])
    sums = [links.start(sum_z_ref.at[zl], sum_z_ref.at[zl], sum_z_ref.at[1 - zl], mate, col)]
    for df in order[:2]:
        gather_n.relay_seconds(df)
    for df in order:
        gather_c.end_second(df)
    for copy in sums:
        copy.wait_recv()
    sum_all_ref[col] = sum_z_ref[0] + sum_z_ref[1]
    sums = [
        links.start(sum_all_ref.at[col], sum_all_ref.at[col], sum_all_ref.at[source], row, peer)
        for peer, source in zip(peers, sources)
    ]
    for df in order[2:]:
        gather_n.relay_seconds(df)
    for df in order:
        gather_n.end_second(df)
    for copy in sums:
        copy.wait_recv()
    for j in range(8):
        terms_ref[:, j * 256 : (j + 1) * 256] = sum_all_ref[j]
    gather_c.end()
    gather_n.end()
    for copy in links.sends:
        copy.wait_send()


def exchanged(part, cot, gain, shift, weight_in, weight_out):
    copies = 56 + 2 * 37
    vmem = pl.BlockSpec(memory_space=pltpu.VMEM)
    return pl.pallas_call(
        exchange,
        out_shape=(
            jax.ShapeDtypeStruct((16, 2048), F32),
            jax.ShapeDtypeStruct((16, 128), BF16),
            jax.ShapeDtypeStruct((8, 2048), F32),
            jax.ShapeDtypeStruct((2, 512, 1024), BF16),
            jax.ShapeDtypeStruct((2, 512, 512), BF16),
        ),
        in_specs=[vmem] * 6,
        out_specs=(vmem,) * 5,
        scratch_shapes=[
            pltpu.VMEM((7, 16, 256), F32),
            pltpu.VMEM((8, 16, 256), F32),
            pltpu.VMEM((8, 16, 256), F32),
            pltpu.VMEM((8, 16, 256), F32),
            pltpu.VMEM((7, 16, 256), F32),
            pltpu.VMEM((8, 16, 128), F32),
            pltpu.VMEM((7, 16, 128), F32),
            pltpu.VMEM((8, 16, 256), F32),
            pltpu.VMEM((4, 8, 256), F32),
            pltpu.VMEM((4, 8, 256), F32),
            pltpu.VMEM((2, 8, 256), F32),
            pltpu.VMEM((8, 8, 256), F32),
            pltpu.SemaphoreType.DMA((copies,)),
            pltpu.SemaphoreType.DMA((copies,)),
            pltpu.SemaphoreType.DMA,
        ],
        compiler_params=pltpu.CompilerParams(
            collective_id=0, has_side_effects=True, vmem_limit_bytes=40 * 1024 * 1024
        ),
    )(part, cot, gain, shift, weight_in, weight_out)


def on_device(features, projection, norm_gain, norm_shift, weight_in, weight_out, cotangent):
    batch = features.shape[0]
    embeds = features.shape[1]
    reduced = jnp.einsum(
        "bnd,nk->bdk", features, projection, preferred_element_type=F32
    ).astype(BF16)
    part = jnp.einsum("bnd,bdk->bnk", features, reduced, preferred_element_type=F32)
    part = part.reshape(batch, 8, 256).transpose(1, 0, 2)
    wide_out = weight_out.reshape(weight_out.shape[0], -1)
    dinter, mixed, terms, rows, cots = exchanged(
        part,
        cotangent.reshape(batch, -1),
        norm_gain.reshape(1, -1),
        norm_shift.reshape(1, -1),
        weight_in,
        wide_out,
    )
    dinter = dinter.reshape(batch, embeds, -1)
    dreduced = jnp.einsum("bnd,bnk->bdk", features, dinter, preferred_element_type=F32)
    grad_features = jnp.einsum("bnk,bdk->bnd", dinter, reduced, preferred_element_type=F32)
    grad_features = grad_features + jnp.einsum(
        "nk,bdk->bnd", projection, dreduced, preferred_element_type=F32
    )

    win = weight_in.reshape(2, 1024, -1)
    wout = wide_out.reshape(-1, 2, 512)
    pre = jnp.einsum("jri,jih->rh", rows, win, preferred_element_type=F32)
    dact = jnp.einsum("jrd,hjd->rh", cots, wout, preferred_element_type=F32)
    sigma = jax.nn.sigmoid(pre)
    act = (pre * sigma).astype(BF16)
    dpre = (dact * sigma * (1.0 + pre * (1.0 - sigma))).astype(BF16)
    grad_in = jnp.einsum("jri,rh->jih", rows, dpre, preferred_element_type=F32).astype(BF16)
    grad_out = jnp.einsum("rh,jrd->hjd", act, cots, preferred_element_type=F32).astype(BF16)
    return (
        mixed.reshape(batch, 1, -1),
        grad_features.astype(BF16),
        terms[0],
        terms[1],
        grad_in.reshape(weight_in.shape),
        grad_out.reshape(weight_out.shape),
    )


def solution(mesh):
    placed = (
        P("row", None, "col"),
        P(),
        P(),
        P(),
        P(None, "col"),
        P("col", None, None),
        P("row", None, "col"),
    )
    return jax.shard_map(
        on_device,
        mesh=mesh,
        in_specs=placed,
        out_specs=(
            P("row", None, "col"),
            P("row", None, "col"),
            P(),
            P(),
            P(None, "col"),
            P("col", None, None),
        ),
        check_vma=False,
    )
```

```python
import jax
import jax.numpy as jnp
from jax import lax
from jax.experimental import pallas as pl
from jax.experimental.pallas import tpu as pltpu
from jax.sharding import PartitionSpec as P

MESH = pl.DeviceIdType.MESH
F32 = jnp.float32
BF16 = jnp.bfloat16
NT = (((1,), (1,)), ((), ()))
TN = (((0,), (0,)), ((), ()))


def mm(a, b, dims=(((1,), (0,)), ((), ()))):
    return lax.dot_general(a, b, dims, preferred_element_type=F32)


class Links:
    def __init__(self, send_sems, recv_sems):
        self.send_sems = send_sems
        self.recv_sems = recv_sems
        self.count = 0
        self.sends = []

    def start(self, src, dst, land, row, col):
        i = self.count
        self.count += 1

        def copy(a, b):
            return pltpu.make_async_remote_copy(
                src_ref=a,
                dst_ref=b,
                send_sem=self.send_sems.at[i],
                recv_sem=self.recv_sems.at[i],
                device_id={"row": row, "col": col},
                device_id_type=MESH,
            )

        out = copy(src, dst)
        out.start()
        self.sends.append(out)
        return copy(land, land)


class Gather:
    def __init__(self, links, buf, where):
        self.links = links
        self.buf = buf
        self.x, self.y, self.zl, self.core, self.row, self.col = where
        self.first = {}
        self.second = {}
        self.sibling = []

    def pos(self, core, df, ds):
        f = (1 - core) * self.x + core * self.y
        s = (1 - core) * self.y + core * self.x
        f = lax.rem(f + df + 4, 4)
        s = lax.rem(s + ds + 4, 4)
        return (1 - core) * (s * 4 + f) + core * (f * 4 + s)

    def block(self, df, ds, zl=None, core=None):
        core = self.core if core is None else core
        p = self.pos(core, df, ds) * 32
        if zl is None:
            return self.buf.at[core, pl.ds(pl.multiple_of(p, 32), 32), :]
        return self.buf.at[core, pl.ds(pl.multiple_of(p + zl * 16, 16), 16), :]

    def start_first(self):
        mine = self.block(0, 0, self.zl)
        for df, other in ((0, 1), (1, 0), (-1, 0), (1, 1), (-1, 1), (2, 0), (2, 1)):
            zl = self.zl + other * (1 - 2 * self.zl)
            to = zl * 16 + self.pos(self.core, df, 0)
            self.first[df, other] = self.links.start(
                mine, mine, self.block(-df if df != 2 else 2, 0, zl), to, self.col
            )

    def to_sibling(self, df, ds, zl=None):
        mine = self.block(df, ds, zl)
        self.sibling.append(
            self.links.start(
                mine,
                mine,
                self.block(df, ds, zl, core=1 - self.core),
                self.row,
                self.col + 1 - 2 * self.core,
            )
        )

    def start_second(self, df):
        back = -df if df != 2 else 2
        for other in (0, 1):
            if (back, other) in self.first:
                self.first[back, other].wait_recv()
        mine = self.block(df, 0)
        for ds in (1, -1, 2):
            to = self.zl * 16 + self.pos(self.core, 0, ds)
            self.second[df, ds] = self.links.start(
                mine, mine, self.block(df, -ds if ds != 2 else 2), to, self.col
            )
        self.to_sibling(df, 0, None if df else 1 - self.zl)

    def end_second(self, df):
        for ds in (1, -1, 2):
            self.second[df, ds].wait_recv()
            self.to_sibling(df, -ds if ds != 2 else 2)

    def end(self):
        for copy in self.sibling:
            copy.wait_recv()


def rows_of(count, width):
    return lax.broadcasted_iota(jnp.int32, (count, width), 0)


def step(
    feat_hbm, proj_ref, gain_ref, shift_ref, win_hbm, wout_hbm, cot_ref,
    mixed_ref, gfeat_ref, gain_out_ref, shift_out_ref, gwin_ref, gwout_ref,
    feat_ref, win_ref, wout_ref, wink_ref, rows_ref, cots_ref, perm_ref,
    part_ref, half_ref, send_ref, got_ref, inter_ref, unit_ref,
    dpart_ref, dhalf_ref, dsend_ref, dgot_ref, dinter_ref,
    out_ref, got_out_ref, terms_ref, term_half_ref, term_z_ref, term_x_ref, term_y_ref, term_all_ref,
    act_ref, dpre_ref, dact_ref, send_sems, recv_sems, local_sems,
):
    row = lax.axis_index("row")
    col = lax.axis_index("col")
    x = lax.rem(row, 4)
    y = lax.rem(row // 4, 4)
    zl = row // 16
    core = lax.rem(col, 2)
    sibling = col + 1 - 2 * core
    mine = core * 4
    other = 4 - mine
    peers = [lax.rem(col + k, 8) for k in range(1, 8)]
    sources = [lax.rem(col + 8 - k, 8) for k in range(1, 8)]
    xs = [y * 4 + lax.rem(x + k, 4) for k in range(1, 4)]
    ys = [lax.rem(y + k, 4) * 4 + x for k in range(1, 4)]
    place = y * 4 + x
    mate = (1 - zl) * 16 + place

    barrier = pltpu.get_barrier_semaphore()

    def greet(to_row, to_col):
        pl.semaphore_signal(barrier, inc=1, device_id={"row": to_row, "col": to_col}, device_id_type=MESH)

    for peer in peers:
        greet(row, peer)
    for p in xs + ys:
        greet(zl * 16 + p, col)
    firsts = [(1 - core) * a + core * b for a, b in zip(xs, ys)]
    for p in firsts:
        greet((1 - zl) * 16 + p, col)
    greet(mate, col)
    for k in (1, 3, 5):
        greet(mate, peers[k])

    here = pl.ds(pl.multiple_of(place * 32 + zl * 16, 16), 16)

    def cot_place(c):
        return cots_ref.at[c // 4, here, pl.ds(pl.multiple_of(lax.rem(c, 4) * 128, 128), 128)]

    loads = [
        pltpu.make_async_copy(feat_hbm.at[pl.ds(4 * i, 4)], feat_ref.at[pl.ds(4 * i, 4)], local_sems.at[i])
        for i in range(4)
    ]
    loads.append(pltpu.make_async_copy(cot_ref, cot_place(col), local_sems.at[4]))
    loads.append(pltpu.make_async_copy(win_hbm, win_ref, local_sems.at[5]))
    loads.append(pltpu.make_async_copy(wout_hbm, wout_ref, local_sems.at[6]))
    for copy in loads:
        copy.start()

    batch = lax.rem(rows_of(64, 512), 16)
    batch_d = lax.rem(rows_of(64, 128), 16)
    pick = (rows_of(64, 4) // 16 == lax.broadcasted_iota(jnp.int32, (64, 4), 1)).astype(F32).astype(BF16)
    proj = mm(pick, proj_ref[...], NT)
    r = rows_of(512, 512)
    perm_ref[...] = (
        (lax.broadcasted_iota(jnp.int32, (512, 512), 1) == lax.rem(r, 128) * 4 + r // 128).astype(F32).astype(BF16)
    )

    def pair(q):
        return jnp.concatenate([feat_ref[2 * q], feat_ref[2 * q + 1]], axis=1)

    def by_features(left):
        total = jnp.zeros((64, 256), F32)
        for q in range(8):
            total = total + mm(jnp.where(batch // 2 == q, left, 0.0).astype(BF16), pair(q))
        return jnp.where(lax.rem(batch_d, 2) == 0, total[:, :128], total[:, 128:])

    def spread(value, q):
        return jnp.concatenate(
            [jnp.where(batch_d == 2 * q + i, value, 0.0) for i in range(2)], axis=1
        ).astype(BF16)

    for copy in loads[:4]:
        copy.wait()
    reduced = by_features(proj).astype(BF16).astype(F32)
    inter = jnp.zeros((64, 512), F32)
    for q in range(8):
        inter = inter + mm(spread(reduced, q), pair(q), NT)
    blocks = [inter[16 * (j // 2) : 16 * (j // 2) + 16, 256 * (j % 2) : 256 * (j % 2) + 256] for j in range(8)]
    total = blocks[0]
    for j in range(1, 8):
        total = total + blocks[j]
    mean = jnp.sum(total, axis=1, keepdims=True) * (1.0 / 2048)
    for j in range(8):
        part_ref[j] = blocks[j] - mean

    pl.semaphore_wait(barrier, 20)
    links = Links(send_sems, recv_sems)
    where = (x, y, zl, core, row, col)
    gather_n = Gather(links, rows_ref, where)
    gather_c = Gather(links, cots_ref, where)

    def fold(parts, landing, sending, landed):
        copy = links.start(parts.at[pl.ds(other, 4)], landing, landing, row, sibling)
        yield
        copy.wait_recv()
        for j in range(4):
            sending[j] = (parts[mine + j] + landing[j]).astype(BF16)
        copies = [links.start(sending, landed.at[k], landed.at[k], row, peers[2 * k + 1]) for k in range(3)]
        yield
        for copy in copies:
            copy.wait_recv()

    fold_inter = fold(part_ref, half_ref, send_ref, got_ref)
    next(fold_inter)
    loads[4].wait()
    slices = [
        links.start(cot_ref, cot_place(col), cot_place(source), row, peer)
        for peer, source in zip(peers, sources)
    ]
    next(fold_inter)

    loads[5].wait()
    for J in range(4):
        moved = mm(perm_ref[...], win_ref[512 * J : 512 * J + 512, :]).astype(BF16)
        for k in range(4):
            wink_ref[k * 512 + J * 128 : k * 512 + J * 128 + 128, :] = moved[k * 128 : k * 128 + 128, :]
    both = jnp.concatenate([gain_ref[...], shift_ref[...]], axis=0)
    moved = [mm(both[:, 512 * J : 512 * J + 512], perm_ref[...], NT) for J in range(4)]
    gains = []
    shifts = []
    for j in range(8):
        k, h = j // 2, j % 2
        wide = jnp.concatenate([moved[2 * h + i][:, 128 * k : 128 * k + 128] for i in range(2)], axis=1)
        gains.append(wide[0:1])
        shifts.append(wide[1:2])

    for copy in slices:
        copy.wait_recv()
    gather_c.start_first()
    loads[6].wait()
    dact = jnp.zeros((16, 512), F32)
    for half in range(2):
        dact = dact + mm(cots_ref[half, here, :], wout_ref[:, half * 512 : (half + 1) * 512], NT)

    next(fold_inter, None)
    for j in range(4):
        inter_ref[mine + j] = (send_ref[j].astype(F32) + got_ref[0, j].astype(F32)) + (
            got_ref[1, j].astype(F32) + got_ref[2, j].astype(F32)
        )
    half = inter_ref.at[pl.ds(mine, 4)]
    copy = links.start(half, half, inter_ref.at[pl.ds(other, 4)], row, sibling)
    copy.wait_recv()

    total = inter_ref[0]
    for j in range(1, 8):
        total = total + inter_ref[j]
    mean = jnp.sum(total, axis=1, keepdims=True) * (1.0 / 2048)
    square = jnp.zeros((16, 256), F32)
    for j in range(8):
        centered = inter_ref[j] - mean
        square = square + centered * centered
    rstd = lax.rsqrt(jnp.sum(square, axis=1, keepdims=True) * (1.0 / 2048) + 1e-05)
    normed = []
    for j in range(8):
        unit = (inter_ref[j] - mean) * rstd
        unit_ref[j] = unit
        normed.append((unit * gains[j] + shifts[j]).astype(BF16))
    stacked = jnp.concatenate(
        [
            jnp.concatenate(
                [normed[2 * k + J // 2][:, 128 * (J % 2) : 128 * (J % 2) + 128] for k in range(4)], axis=1
            )
            for J in range(4)
        ],
        axis=0,
    )
    natural = mm(stacked, perm_ref[...]).astype(BF16)
    for J in range(4):
        rows_ref[J // 2, here, 512 * (J % 2) : 512 * (J % 2) + 512] = natural[16 * J : 16 * J + 16, :]
    gather_n.start_first()

    pre = jnp.zeros((16, 512), F32)
    for j in range(8):
        pre = pre + mm(normed[j], wink_ref[j * 256 : (j + 1) * 256, :])
    sigma = 1.0 / (1.0 + jnp.exp(-pre))
    act = (pre * sigma).astype(BF16)
    dpre = (dact * sigma * (1.0 + pre * (1.0 - sigma))).astype(BF16)
    first = jnp.zeros((16, 256), F32)
    second = jnp.zeros((16, 256), F32)
    gain_terms = []
    shift_terms = []
    scaled = []
    for j in range(8):
        dnormed = mm(dpre, wink_ref[j * 256 : (j + 1) * 256, :], NT)
        gain_terms.append(jnp.sum(dnormed * unit_ref[j], axis=0, keepdims=True))
        shift_terms.append(jnp.sum(dnormed, axis=0, keepdims=True))
        scaled.append(dnormed * gains[j])
        first = first + scaled[j]
        second = second + scaled[j] * unit_ref[j]
    first = jnp.sum(first, axis=1, keepdims=True) * (1.0 / 2048)
    second = jnp.sum(second, axis=1, keepdims=True) * (1.0 / 2048)
    for j in range(8):
        dpart_ref[j] = rstd * (scaled[j] - first - unit_ref[j] * second)
    fold_dinter = fold(dpart_ref, dhalf_ref, dsend_ref, dgot_ref)
    next(fold_dinter)
    for h in range(2):
        terms_ref[h] = jnp.concatenate(gain_terms[4 * h : 4 * h + 4] + shift_terms[4 * h : 4 * h + 4], axis=0)
    term = links.start(terms_ref.at[1 - core], term_half_ref, term_half_ref, row, sibling)
    next(fold_dinter)

    def z_of(r, c):
        return (c // 2) * 2 + r // 16

    term.wait_recv()
    at = z_of(row, col)
    term_z_ref[at] = terms_ref[core] + term_half_ref[...]
    terms = []
    for k in range(4):
        for r in (row, mate):
            if k or r is mate:
                to = lax.rem(col + 2 * k, 8)
                source = lax.rem(col + 8 - 2 * k, 8)
                terms.append(
                    links.start(term_z_ref.at[at], term_z_ref.at[at], term_z_ref.at[z_of(r, source)], r, to)
                )
    for j in range(8):
        out_ref[j] = mm(act, wout_ref[:, j * 128 : (j + 1) * 128])
    outs = [
        links.start(out_ref.at[peer], got_out_ref.at[k], got_out_ref.at[k], row, peer)
        for k, peer in enumerate(peers)
    ]
    order = (0, 1, -1, 2)
    for df in order:
        gather_c.start_second(df)
    for df in order:
        gather_n.start_second(df)
    for df in order:
        gather_c.end_second(df)

    next(fold_dinter, None)
    for j in range(4):
        dinter_ref[mine + j] = (
            (dsend_ref[j].astype(F32) + dgot_ref[0, j].astype(F32))
            + (dgot_ref[1, j].astype(F32) + dgot_ref[2, j].astype(F32))
        ).astype(BF16)
    half = dinter_ref.at[pl.ds(mine, 4)]
    copy = links.start(half, half, dinter_ref.at[pl.ds(other, 4)], row, sibling)
    for term in terms:
        term.wait_recv()
    total = term_z_ref[0]
    for k in range(1, 8):
        total = total + term_z_ref[k]
    term_x_ref[x] = total
    terms = [
        links.start(term_x_ref.at[x], term_x_ref.at[x], term_x_ref.at[lax.rem(x + 4 - k, 4)], zl * 16 + xs[k - 1], col)
        for k in range(1, 4)
    ]
    copy.wait_recv()
    dinter = jnp.concatenate(
        [jnp.concatenate([dinter_ref[2 * k], dinter_ref[2 * k + 1]], axis=1) for k in range(4)], axis=0
    ).astype(F32)
    dreduced = by_features(dinter)
    left = jnp.transpose(jnp.concatenate([dinter, proj], axis=0)).astype(BF16)
    for q in range(8):
        right = jnp.concatenate([spread(reduced, q), spread(dreduced, q)], axis=0)
        grad = mm(left, right).astype(BF16)
        gfeat_ref[2 * q] = grad[:, :128]
        gfeat_ref[2 * q + 1] = grad[:, 128:]

    for term in terms:
        term.wait_recv()
    term_y_ref[y] = (term_x_ref[0] + term_x_ref[1]) + (term_x_ref[2] + term_x_ref[3])
    terms = [
        links.start(term_y_ref.at[y], term_y_ref.at[y], term_y_ref.at[lax.rem(y + 4 - k, 4)], zl * 16 + ys[k - 1], col)
        for k in range(1, 4)
    ]
    mixed = out_ref[col]
    for k, copy in enumerate(outs):
        copy.wait_recv()
        mixed = mixed + got_out_ref[k]
    mixed_ref[...] = mixed.astype(BF16)

    for df in order:
        gather_n.end_second(df)
    gather_c.end()

    def dacts(i, carry):
        at = pl.ds(pl.multiple_of(i * 256, 256), 256)
        dact_ref[at, :] = mm(cots_ref[0, at, :], wout_ref[:, :512], NT) + mm(
            cots_ref[1, at, :], wout_ref[:, 512:], NT
        )
        return carry

    lax.fori_loop(0, 2, dacts, 0)
    for term in terms:
        term.wait_recv()
    term_all_ref[core] = (term_y_ref[0] + term_y_ref[1]) + (term_y_ref[2] + term_y_ref[3])
    term = links.start(term_all_ref.at[core], term_all_ref.at[core], term_all_ref.at[1 - core], row, sibling)
    gather_n.end()

    def hidden(i, carry):
        at = pl.ds(pl.multiple_of(i * 256, 256), 256)
        pre = mm(rows_ref[0, at, :], win_ref[:1024, :]) + mm(rows_ref[1, at, :], win_ref[1024:, :])
        sigma = 1.0 / (1.0 + jnp.exp(-pre))
        act_ref[at, :] = (pre * sigma).astype(BF16)
        dpre_ref[at, :] = (dact_ref[at, :] * sigma * (1.0 + pre * (1.0 - sigma))).astype(BF16)
        return carry

    lax.fori_loop(0, 2, hidden, 0)

    def grads_in(i, carry):
        at = pl.ds(pl.multiple_of(i * 256, 256), 256)
        columns = pl.ds(pl.multiple_of(lax.rem(i, 4) * 256, 256), 256)
        gwin_ref[at, :] = mm(rows_ref[i // 4, :, columns], dpre_ref[...], TN).astype(BF16)
        return carry

    lax.fori_loop(0, 8, grads_in, 0)
    for half in range(2):
        gwout_ref[:, half * 512 : (half + 1) * 512] = mm(act_ref[...], cots_ref[half], TN).astype(BF16)

    term.wait_recv()
    lines = []
    for J in range(4):
        for base in (0, 4):
            lines.append(
                jnp.concatenate(
                    [
                        term_all_ref[
                            k // 2,
                            base + 2 * (k % 2) + J // 2 : base + 2 * (k % 2) + J // 2 + 1,
                            128 * (J % 2) : 128 * (J % 2) + 128,
                        ]
                        for k in range(4)
                    ],
                    axis=1,
                )
            )
    rest = jnp.concatenate(lines, axis=0)
    total = jnp.zeros((8, 512), F32)
    for _ in range(3):
        piece = rest.astype(BF16)
        rest = rest - piece.astype(F32)
        total = total + mm(piece, perm_ref[...])
    for J in range(4):
        gain_out_ref[:, J * 512 : J * 512 + 512] = total[2 * J : 2 * J + 1, :]
        shift_out_ref[:, J * 512 : J * 512 + 512] = total[2 * J + 1 : 2 * J + 2, :]
    for copy in links.sends:
        copy.wait_send()


def on_device(features, projection, norm_gain, norm_shift, weight_in, weight_out, cotangent):
    copies = 130
    vmem = pl.BlockSpec(memory_space=pltpu.VMEM)
    hbm = pl.BlockSpec(memory_space=pl.ANY)
    mixed, gfeat, gain, shift, gwin, gwout = pl.pallas_call(
        step,
        out_shape=(
            jax.ShapeDtypeStruct((16, 128), BF16),
            jax.ShapeDtypeStruct((16, 512, 128), BF16),
            jax.ShapeDtypeStruct((1, 2048), F32),
            jax.ShapeDtypeStruct((1, 2048), F32),
            jax.ShapeDtypeStruct((2048, 512), BF16),
            jax.ShapeDtypeStruct((512, 1024), BF16),
        ),
        in_specs=[hbm, vmem, vmem, vmem, hbm, hbm, vmem],
        out_specs=(vmem,) * 6,
        scratch_shapes=[
            pltpu.VMEM((16, 512, 128), BF16),
            pltpu.VMEM((2048, 512), BF16),
            pltpu.VMEM((512, 1024), BF16),
            pltpu.VMEM((2048, 512), BF16),
            pltpu.VMEM((2, 512, 1024), BF16),
            pltpu.VMEM((2, 512, 512), BF16),
            pltpu.VMEM((512, 512), BF16),
            pltpu.VMEM((8, 16, 256), F32),
            pltpu.VMEM((4, 16, 256), F32),
            pltpu.VMEM((4, 16, 256), BF16),
            pltpu.VMEM((3, 4, 16, 256), BF16),
            pltpu.VMEM((8, 16, 256), F32),
            pltpu.VMEM((8, 16, 256), F32),
            pltpu.VMEM((8, 16, 256), F32),
            pltpu.VMEM((4, 16, 256), F32),
            pltpu.VMEM((4, 16, 256), BF16),
            pltpu.VMEM((3, 4, 16, 256), BF16),
            pltpu.VMEM((8, 16, 256), BF16),
            pltpu.VMEM((8, 16, 128), F32),
            pltpu.VMEM((7, 16, 128), F32),
            pltpu.VMEM((2, 8, 256), F32),
            pltpu.VMEM((8, 256), F32),
            pltpu.VMEM((8, 8, 256), F32),
            pltpu.VMEM((4, 8, 256), F32),
            pltpu.VMEM((4, 8, 256), F32),
            pltpu.VMEM((2, 8, 256), F32),
            pltpu.VMEM((512, 512), BF16),
            pltpu.VMEM((512, 512), BF16),
            pltpu.VMEM((512, 512), F32),
            pltpu.SemaphoreType.DMA((copies,)),
            pltpu.SemaphoreType.DMA((copies,)),
            pltpu.SemaphoreType.DMA((7,)),
        ],
        compiler_params=pltpu.CompilerParams(
            collective_id=0, has_side_effects=True, vmem_limit_bytes=48 * 1024 * 1024
        ),
    )(
        features,
        projection,
        norm_gain.reshape(1, -1),
        norm_shift.reshape(1, -1),
        weight_in,
        weight_out.reshape(weight_out.shape[0], -1),
        cotangent.reshape(cotangent.shape[0], -1),
    )
    return (
        mixed.reshape(cotangent.shape),
        gfeat,
        gain.reshape(-1),
        shift.reshape(-1),
        gwin,
        gwout.reshape(weight_out.shape),
    )


def solution(mesh):
    placed = (
        P("row", None, "col"),
        P(),
        P(),
        P(),
        P(None, "col"),
        P("col", None, None),
        P("row", None, "col"),
    )
    return jax.shard_map(
        on_device,
        mesh=mesh,
        in_specs=placed,
        out_specs=(
            P("row", None, "col"),
            P("row", None, "col"),
            P(),
            P(),
            P(None, "col"),
            P("col", None, None),
        ),
        check_vma=False,
    )
```

```python
import jax
import jax.numpy as jnp
from jax import lax
from jax.experimental import pallas as pl
from jax.experimental.pallas import tpu as pltpu
from jax.sharding import PartitionSpec as P

MESH = pl.DeviceIdType.MESH
F32 = jnp.float32
BF16 = jnp.bfloat16
NT = (((1,), (1,)), ((), ()))
TN = (((0,), (0,)), ((), ()))


def mm(a, b, dims=(((1,), (0,)), ((), ()))):
    return lax.dot_general(a, b, dims, preferred_element_type=F32)


class Links:
    def __init__(self, send_sems, recv_sems):
        self.send_sems = send_sems
        self.recv_sems = recv_sems
        self.count = 0
        self.sends = []

    def start(self, src, dst, land, row, col):
        i = self.count
        self.count += 1

        def copy(a, b):
            return pltpu.make_async_remote_copy(
                src_ref=a,
                dst_ref=b,
                send_sem=self.send_sems.at[i],
                recv_sem=self.recv_sems.at[i],
                device_id={"row": row, "col": col},
                device_id_type=MESH,
            )

        out = copy(src, dst)
        out.start()
        self.sends.append(out)
        return copy(land, land)


class Gather:
    def __init__(self, links, buf, where):
        self.links = links
        self.buf = buf
        self.x, self.y, self.zl, self.core, self.row, self.col = where
        self.first = {}
        self.second = {}
        self.sibling = []

    def pos(self, core, df, ds):
        f = (1 - core) * self.x + core * self.y
        s = (1 - core) * self.y + core * self.x
        f = lax.rem(f + df + 4, 4)
        s = lax.rem(s + ds + 4, 4)
        return (1 - core) * (s * 4 + f) + core * (f * 4 + s)

    def block(self, df, ds, zl=None, core=None):
        core = self.core if core is None else core
        p = self.pos(core, df, ds) * 32
        if zl is None:
            return self.buf.at[core, pl.ds(pl.multiple_of(p, 32), 32), :]
        return self.buf.at[core, pl.ds(pl.multiple_of(p + zl * 16, 16), 16), :]

    def start_first(self):
        mine = self.block(0, 0, self.zl)
        for df, other in ((0, 1), (1, 0), (-1, 0), (1, 1), (-1, 1), (2, 0), (2, 1)):
            zl = self.zl + other * (1 - 2 * self.zl)
            to = zl * 16 + self.pos(self.core, df, 0)
            self.first[df, other] = self.links.start(
                mine, mine, self.block(-df if df != 2 else 2, 0, zl), to, self.col
            )

    def to_sibling(self, df, ds, zl=None):
        mine = self.block(df, ds, zl)
        self.sibling.append(
            self.links.start(
                mine,
                mine,
                self.block(df, ds, zl, core=1 - self.core),
                self.row,
                self.col + 1 - 2 * self.core,
            )
        )

    def start_second(self, df):
        back = -df if df != 2 else 2
        for other in (0, 1):
            if (back, other) in self.first:
                self.first[back, other].wait_recv()
        mine = self.block(df, 0)
        for ds in (1, -1, 2):
            to = self.zl * 16 + self.pos(self.core, 0, ds)
            self.second[df, ds] = self.links.start(
                mine, mine, self.block(df, -ds if ds != 2 else 2), to, self.col
            )
        self.to_sibling(df, 0, None if df else 1 - self.zl)

    def end_second(self, df):
        for ds in (1, -1, 2):
            self.second[df, ds].wait_recv()
            self.to_sibling(df, -ds if ds != 2 else 2)

    def end(self):
        for copy in self.sibling:
            copy.wait_recv()


def rows_of(count, width):
    return lax.broadcasted_iota(jnp.int32, (count, width), 0)


def step(
    feat_hbm, proj_hbm, gain_hbm, shift_hbm, win_hbm, wout_hbm, cot_hbm,
    mixed_ref, gfeat_hbm, gain_out_ref, shift_out_ref, gwin_hbm, gwout_hbm,
    feat_ref, proj_ref, norm_ref, win_ref, wout_ref, wink_ref, rows_ref, cots_ref, perm_ref,
    part_ref, half_ref, send_ref, got_ref, inter_ref, unit_ref,
    dpart_ref, dhalf_ref, dsend_ref, dgot_ref, dinter_ref,
    out_ref, got_out_ref, terms_ref, term_half_ref, term_z_ref, term_x_ref, term_y_ref, term_all_ref,
    act_ref, dpre_ref, dact_ref, gfeat_ref, gwin_ref, gwout_ref,
    send_sems, recv_sems, local_sems, store_sems,
):
    row = lax.axis_index("row")
    col = lax.axis_index("col")
    x = lax.rem(row, 4)
    y = lax.rem(row // 4, 4)
    zl = row // 16
    core = lax.rem(col, 2)
    sibling = col + 1 - 2 * core
    mine = core * 4
    other = 4 - mine
    peers = [lax.rem(col + k, 8) for k in range(1, 8)]
    sources = [lax.rem(col + 8 - k, 8) for k in range(1, 8)]
    xs = [y * 4 + lax.rem(x + k, 4) for k in range(1, 4)]
    ys = [lax.rem(y + k, 4) * 4 + x for k in range(1, 4)]
    place = y * 4 + x
    mate = (1 - zl) * 16 + place

    barrier = pltpu.get_barrier_semaphore()

    def greet(to_row, to_col):
        pl.semaphore_signal(barrier, inc=1, device_id={"row": to_row, "col": to_col}, device_id_type=MESH)

    here = pl.ds(pl.multiple_of(place * 32 + zl * 16, 16), 16)

    def cot_place(c):
        return cots_ref.at[c // 4, here, pl.ds(pl.multiple_of(lax.rem(c, 4) * 128, 128), 128)]

    loads = [
        pltpu.make_async_copy(feat_hbm.at[pl.ds(4 * i, 4)], feat_ref.at[pl.ds(4 * i, 4)], local_sems.at[i])
        for i in range(4)
    ]
    loads.append(pltpu.make_async_copy(cot_hbm, cot_place(col), local_sems.at[4]))
    loads.append(pltpu.make_async_copy(win_hbm, win_ref, local_sems.at[5]))
    loads.append(pltpu.make_async_copy(wout_hbm, wout_ref, local_sems.at[6]))
    loads.append(pltpu.make_async_copy(gain_hbm, norm_ref.at[0], local_sems.at[7]))
    loads.append(pltpu.make_async_copy(shift_hbm, norm_ref.at[1], local_sems.at[8]))
    load_proj = pltpu.make_async_copy(proj_hbm, proj_ref, local_sems.at[9])
    load_proj.start()
    for copy in loads[:5]:
        copy.start()

    for peer in peers:
        greet(row, peer)
    for p in xs + ys:
        greet(zl * 16 + p, col)
    firsts = [(1 - core) * a + core * b for a, b in zip(xs, ys)]
    for p in firsts:
        greet((1 - zl) * 16 + p, col)
    greet(mate, col)
    for k in (1, 3, 5):
        greet(mate, peers[k])

    batch = rows_of(64, 512) & 15
    batch_d = rows_of(64, 128) & 15
    pick = (rows_of(64, 4) >> 4 == lax.broadcasted_iota(jnp.int32, (64, 4), 1)).astype(F32).astype(BF16)
    load_proj.wait()
    proj = mm(pick, proj_ref[...])
    r = rows_of(512, 512)
    perm_ref[...] = (
        (lax.broadcasted_iota(jnp.int32, (512, 512), 1) == (r & 127) * 4 + (r >> 7)).astype(F32).astype(BF16)
    )

    def pair(q):
        return jnp.concatenate([feat_ref[2 * q], feat_ref[2 * q + 1]], axis=1)

    def by_features(left):
        total = jnp.zeros((64, 256), F32)
        for q in range(8):
            total = total + mm(jnp.where(batch >> 1 == q, left, 0.0).astype(BF16), pair(q))
        return jnp.where(batch_d & 1 == 0, total[:, :128], total[:, 128:])

    def spread(value, q):
        return jnp.concatenate(
            [jnp.where(batch_d == 2 * q + i, value, 0.0) for i in range(2)], axis=1
        ).astype(BF16)

    for copy in loads[:4]:
        copy.wait()
    for copy in loads[5:]:
        copy.start()
    reduced = by_features(proj).astype(BF16).astype(F32)
    inter = jnp.zeros((64, 512), F32)
    for q in range(8):
        inter = inter + mm(spread(reduced, q), pair(q), NT)
    blocks = [inter[16 * (j // 2) : 16 * (j // 2) + 16, 256 * (j % 2) : 256 * (j % 2) + 256] for j in range(8)]
    total = blocks[0]
    for j in range(1, 8):
        total = total + blocks[j]
    mean = jnp.sum(total, axis=1, keepdims=True) * (1.0 / 2048)
    for j in range(8):
        part_ref[j] = blocks[j] - mean

    pl.semaphore_wait(barrier, 20)
    links = Links(send_sems, recv_sems)
    where = (x, y, zl, core, row, col)
    gather_n = Gather(links, rows_ref, where)
    gather_c = Gather(links, cots_ref, where)

    def fold(parts, landing, sending, landed):
        copy = links.start(parts.at[pl.ds(other, 4)], landing, landing, row, sibling)
        yield
        copy.wait_recv()
        for j in range(4):
            sending[j] = (parts[mine + j] + landing[j]).astype(BF16)
        copies = [links.start(sending, landed.at[k], landed.at[k], row, peers[2 * k + 1]) for k in (1, 0, 2)]
        yield
        for copy in copies:
            copy.wait_recv()

    fold_inter = fold(part_ref, half_ref, send_ref, got_ref)
    next(fold_inter)
    next(fold_inter)
    loads[4].wait()
    slices = [
        links.start(cot_place(col), cot_place(col), cot_place(source), row, peer)
        for peer, source in zip(peers, sources)
    ]

    loads[5].wait()
    for J in range(4):
        moved = mm(perm_ref[...], win_ref[512 * J : 512 * J + 512, :]).astype(BF16)
        for k in range(4):
            wink_ref[k * 512 + J * 128 : k * 512 + J * 128 + 128, :] = moved[k * 128 : k * 128 + 128, :]
    loads[7].wait()
    loads[8].wait()
    lines = jnp.concatenate([norm_ref[0], norm_ref[1]], axis=0)
    take = (rows_of(8, 32) & 3) * 4 + (rows_of(8, 32) >> 2) * 16
    both = jnp.concatenate(
        [
            mm((lax.broadcasted_iota(jnp.int32, (8, 32), 1) == take + i).astype(F32).astype(BF16), lines)
            for i in range(4)
        ],
        axis=1,
    ).astype(BF16)
    moved = mm(both, perm_ref[...], NT)
    gains = []
    shifts = []
    for j in range(8):
        k, h = j // 2, j % 2
        for base, into in ((0, gains), (4, shifts)):
            J = base + 2 * h
            into.append(
                jnp.concatenate([moved[J + i : J + i + 1, 128 * k : 128 * k + 128] for i in range(2)], axis=1)
            )

    for copy in slices:
        copy.wait_recv()
    gather_c.start_first()
    loads[6].wait()
    dact = jnp.zeros((16, 512), F32)
    for half in range(2):
        dact = dact + mm(cots_ref[half, here, :], wout_ref[:, half * 512 : (half + 1) * 512], NT)

    next(fold_inter, None)
    for j in range(4):
        inter_ref[mine + j] = (send_ref[j].astype(F32) + got_ref[0, j].astype(F32)) + (
            got_ref[1, j].astype(F32) + got_ref[2, j].astype(F32)
        )
    half = inter_ref.at[pl.ds(mine, 4)]
    copy = links.start(half, half, inter_ref.at[pl.ds(other, 4)], row, sibling)
    copy.wait_recv()

    total = inter_ref[0]
    for j in range(1, 8):
        total = total + inter_ref[j]
    mean = jnp.sum(total, axis=1, keepdims=True) * (1.0 / 2048)
    square = jnp.zeros((16, 256), F32)
    for j in range(8):
        centered = inter_ref[j] - mean
        square = square + centered * centered
    rstd = lax.rsqrt(jnp.sum(square, axis=1, keepdims=True) * (1.0 / 2048) + 1e-05)
    normed = []
    for j in range(8):
        unit = (inter_ref[j] - mean) * rstd
        unit_ref[j] = unit
        normed.append((unit * gains[j] + shifts[j]).astype(BF16))
    stacked = jnp.concatenate(
        [
            jnp.concatenate(
                [normed[2 * k + J // 2][:, 128 * (J % 2) : 128 * (J % 2) + 128] for k in range(4)], axis=1
            )
            for J in range(4)
        ],
        axis=0,
    )
    natural = mm(stacked, perm_ref[...]).astype(BF16)
    for J in range(4):
        rows_ref[J // 2, here, 512 * (J % 2) : 512 * (J % 2) + 512] = natural[16 * J : 16 * J + 16, :]
    gather_n.start_first()
    order = (0, 1, -1, 2)

    pre = jnp.zeros((16, 512), F32)
    for j in range(8):
        pre = pre + mm(normed[j], wink_ref[j * 256 : (j + 1) * 256, :])
    sigma = 1.0 / (1.0 + jnp.exp(-pre))
    act = (pre * sigma).astype(BF16)
    dpre = (dact * sigma * (1.0 + pre * (1.0 - sigma))).astype(BF16)
    first = jnp.zeros((16, 256), F32)
    second = jnp.zeros((16, 256), F32)
    gain_terms = []
    shift_terms = []
    scaled = []
    for j in range(8):
        dnormed = mm(dpre, wink_ref[j * 256 : (j + 1) * 256, :], NT)
        gain_terms.append(jnp.sum(dnormed * unit_ref[j], axis=0, keepdims=True))
        shift_terms.append(jnp.sum(dnormed, axis=0, keepdims=True))
        scaled.append(dnormed * gains[j])
        first = first + scaled[j]
        second = second + scaled[j] * unit_ref[j]
    first = jnp.sum(first, axis=1, keepdims=True) * (1.0 / 2048)
    second = jnp.sum(second, axis=1, keepdims=True) * (1.0 / 2048)
    for j in range(8):
        dpart_ref[j] = rstd * (scaled[j] - first - unit_ref[j] * second)
    fold_dinter = fold(dpart_ref, dhalf_ref, dsend_ref, dgot_ref)
    next(fold_dinter)
    for h in range(2):
        terms_ref[h] = jnp.concatenate(gain_terms[4 * h : 4 * h + 4] + shift_terms[4 * h : 4 * h + 4], axis=0)
    term = links.start(terms_ref.at[1 - core], term_half_ref, term_half_ref, row, sibling)
    next(fold_dinter)

    def z_of(r, c):
        return (c // 2) * 2 + r // 16

    term.wait_recv()
    at = z_of(row, col)
    term_z_ref[at] = terms_ref[core] + term_half_ref[...]
    terms = []
    for k in range(4):
        for r in (row, mate):
            if k or r is mate:
                to = lax.rem(col + 2 * k, 8)
                source = lax.rem(col + 8 - 2 * k, 8)
                terms.append(
                    links.start(term_z_ref.at[at], term_z_ref.at[at], term_z_ref.at[z_of(r, source)], r, to)
                )
    for j in range(8):
        out_ref[j] = mm(act, wout_ref[:, j * 128 : (j + 1) * 128])
    for df in order:
        gather_c.start_second(df)
    outs = [
        links.start(out_ref.at[peer], got_out_ref.at[k], got_out_ref.at[k], row, peer)
        for k, peer in enumerate(peers)
    ]
    for df in order:
        gather_n.start_second(df)
    for term in terms:
        term.wait_recv()
    total = term_z_ref[0]
    for k in range(1, 8):
        total = total + term_z_ref[k]
    term_x_ref[x] = total
    terms = [
        links.start(term_x_ref.at[x], term_x_ref.at[x], term_x_ref.at[lax.rem(x + 4 - k, 4)], zl * 16 + xs[k - 1], col)
        for k in range(1, 4)
    ]
    for df in order:
        gather_c.end_second(df)

    def dacts(i, carry):
        at = pl.ds(pl.multiple_of(i * 256, 256), 256)
        dact_ref[at, :] = mm(cots_ref[0, at, :], wout_ref[:, :512], NT) + mm(
            cots_ref[1, at, :], wout_ref[:, 512:], NT
        )
        return carry

    gather_c.end()
    lax.fori_loop(0, 2, dacts, 0)
    next(fold_dinter, None)
    for j in range(4):
        dinter_ref[mine + j] = (
            (dsend_ref[j].astype(F32) + dgot_ref[0, j].astype(F32))
            + (dgot_ref[1, j].astype(F32) + dgot_ref[2, j].astype(F32))
        ).astype(BF16)
    half = dinter_ref.at[pl.ds(mine, 4)]
    copy = links.start(half, half, dinter_ref.at[pl.ds(other, 4)], row, sibling)
    copy.wait_recv()
    dinter = jnp.concatenate(
        [jnp.concatenate([dinter_ref[2 * k], dinter_ref[2 * k + 1]], axis=1) for k in range(4)], axis=0
    ).astype(F32)
    dreduced = by_features(dinter)
    stores = []
    left = jnp.transpose(jnp.concatenate([dinter, proj], axis=0)).astype(BF16)
    for q in range(8):
        right = jnp.concatenate([spread(reduced, q), spread(dreduced, q)], axis=0)
        grad = mm(left, right).astype(BF16)
        gfeat_ref[2 * q] = grad[:, :128]
        gfeat_ref[2 * q + 1] = grad[:, 128:]
        if q % 2:
            part = pl.ds(2 * q - 2, 4)
            stores.append(
                pltpu.make_async_copy(gfeat_ref.at[part], gfeat_hbm.at[part], store_sems.at[8 + q // 2])
            )
            stores[-1].start()
            gather_n.end_second(order[q // 2])

    for term in terms:
        term.wait_recv()
    term_y_ref[y] = (term_x_ref[0] + term_x_ref[1]) + (term_x_ref[2] + term_x_ref[3])
    terms = [
        links.start(term_y_ref.at[y], term_y_ref.at[y], term_y_ref.at[lax.rem(y + 4 - k, 4)], zl * 16 + ys[k - 1], col)
        for k in range(1, 4)
    ]
    mixed = out_ref[col]
    for k, copy in enumerate(outs):
        copy.wait_recv()
        mixed = mixed + got_out_ref[k]
    mixed_ref[...] = mixed.astype(BF16)

    gather_n.end()


    def hidden(i, carry):
        at = pl.ds(pl.multiple_of(i * 256, 256), 256)
        pre = mm(rows_ref[0, at, :], win_ref[:1024, :]) + mm(rows_ref[1, at, :], win_ref[1024:, :])
        sigma = 1.0 / (1.0 + jnp.exp(-pre))
        act_ref[at, :] = (pre * sigma).astype(BF16)
        dpre_ref[at, :] = (dact_ref[at, :] * sigma * (1.0 + pre * (1.0 - sigma))).astype(BF16)
        return carry

    lax.fori_loop(0, 2, hidden, 0)
    for term in terms:
        term.wait_recv()
    term_all_ref[core] = (term_y_ref[0] + term_y_ref[1]) + (term_y_ref[2] + term_y_ref[3])
    term = links.start(term_all_ref.at[core], term_all_ref.at[core], term_all_ref.at[1 - core], row, sibling)

    def grads_in(i, carry):
        at = pl.ds(pl.multiple_of(i * 256, 256), 256)
        columns = pl.ds(pl.multiple_of(lax.rem(i, 4) * 256, 256), 256)
        gwin_ref[at, :] = mm(rows_ref[i // 4, :, columns], dpre_ref[...], TN).astype(BF16)
        pltpu.make_async_copy(gwin_ref.at[at, :], gwin_hbm.at[at, :], store_sems.at[i]).start()
        return carry

    lax.fori_loop(0, 8, grads_in, 0)
    for i in range(8):
        at = pl.ds(i * 256, 256)
        stores.append(pltpu.make_async_copy(gwin_ref.at[at, :], gwin_hbm.at[at, :], store_sems.at[i]))

    term.wait_recv()
    lines = []
    for J in range(4):
        for base in (0, 4):
            lines.append(
                jnp.concatenate(
                    [
                        term_all_ref[
                            k // 2,
                            base + 2 * (k % 2) + J // 2 : base + 2 * (k % 2) + J // 2 + 1,
                            128 * (J % 2) : 128 * (J % 2) + 128,
                        ]
                        for k in range(4)
                    ],
                    axis=1,
                )
            )
    rest = jnp.concatenate(lines, axis=0)
    total = jnp.zeros((8, 512), F32)
    for _ in range(3):
        piece = rest.astype(BF16)
        rest = rest - piece.astype(F32)
        total = total + mm(piece, perm_ref[...])
    for J in range(4):
        gain_out_ref[:, J * 512 : J * 512 + 512] = total[2 * J : 2 * J + 1, :]
        shift_out_ref[:, J * 512 : J * 512 + 512] = total[2 * J + 1 : 2 * J + 2, :]
    for half in range(2):
        columns = slice(half * 512, (half + 1) * 512)
        gwout_ref[:, columns] = mm(act_ref[...], cots_ref[half], TN).astype(BF16)
        stores.append(
            pltpu.make_async_copy(gwout_ref.at[:, columns], gwout_hbm.at[:, columns], store_sems.at[12 + half])
        )
        stores[-1].start()
    for copy in links.sends:
        copy.wait_send()
    for copy in stores:
        copy.wait()


def store(*refs):
    sources, targets, held = refs[:6], refs[6:12], refs[12:18]
    loads, stores = [], []
    for source, target, buf in zip(sources, targets, held):
        rows = source.shape[0]
        parts = 4 if rows * source.shape[-1] > 65536 or len(source.shape) == 3 else 1
        for i in range(parts):
            at = pl.ds(i * (rows // parts), rows // parts)
            n = len(loads)
            loads.append(pltpu.make_async_copy(source.at[at], buf.at[at], refs[18].at[n]))
            stores.append(pltpu.make_async_copy(buf.at[at], target.at[at], refs[19].at[n]))
    for copy in loads:
        copy.start()
    for load, save in zip(loads, stores):
        load.wait()
        save.start()
    for save in stores:
        save.wait()


def on_device(features, projection, norm_gain, norm_shift, weight_in, weight_out, cotangent):
    copies = 130
    vmem = pl.BlockSpec(memory_space=pltpu.VMEM)
    hbm = pl.BlockSpec(memory_space=pltpu.HBM)
    results = pl.pallas_call(
        step,
        out_shape=(
            jax.ShapeDtypeStruct((16, 128), BF16),
            jax.ShapeDtypeStruct((16, 512, 128), BF16),
            jax.ShapeDtypeStruct((1, 2048), F32),
            jax.ShapeDtypeStruct((1, 2048), F32),
            jax.ShapeDtypeStruct((2048, 512), BF16),
            jax.ShapeDtypeStruct((512, 1024), BF16),
        ),
        in_specs=[hbm] * 7,
        out_specs=(vmem, hbm, vmem, vmem, hbm, hbm),
        scratch_shapes=[
            pltpu.VMEM((16, 512, 128), BF16),
            pltpu.VMEM((4, 512), BF16),
            pltpu.VMEM((2, 16, 128), BF16),
            pltpu.VMEM((2048, 512), BF16),
            pltpu.VMEM((512, 1024), BF16),
            pltpu.VMEM((2048, 512), BF16),
            pltpu.VMEM((2, 512, 1024), BF16),
            pltpu.VMEM((2, 512, 512), BF16),
            pltpu.VMEM((512, 512), BF16),
            pltpu.VMEM((8, 16, 256), F32),
            pltpu.VMEM((4, 16, 256), F32),
            pltpu.VMEM((4, 16, 256), BF16),
            pltpu.VMEM((3, 4, 16, 256), BF16),
            pltpu.VMEM((8, 16, 256), F32),
            pltpu.VMEM((8, 16, 256), F32),
            pltpu.VMEM((8, 16, 256), F32),
            pltpu.VMEM((4, 16, 256), F32),
            pltpu.VMEM((4, 16, 256), BF16),
            pltpu.VMEM((3, 4, 16, 256), BF16),
            pltpu.VMEM((8, 16, 256), BF16),
            pltpu.VMEM((8, 16, 128), F32),
            pltpu.VMEM((7, 16, 128), F32),
            pltpu.VMEM((2, 8, 256), F32),
            pltpu.VMEM((8, 256), F32),
            pltpu.VMEM((8, 8, 256), F32),
            pltpu.VMEM((4, 8, 256), F32),
            pltpu.VMEM((4, 8, 256), F32),
            pltpu.VMEM((2, 8, 256), F32),
            pltpu.VMEM((512, 512), BF16),
            pltpu.VMEM((512, 512), BF16),
            pltpu.VMEM((512, 512), F32),
            pltpu.VMEM((16, 512, 128), BF16),
            pltpu.VMEM((2048, 512), BF16),
            pltpu.VMEM((512, 1024), BF16),
            pltpu.SemaphoreType.DMA((copies,)),
            pltpu.SemaphoreType.DMA((copies,)),
            pltpu.SemaphoreType.DMA((10,)),
            pltpu.SemaphoreType.DMA((14,)),
        ],
        compiler_params=pltpu.CompilerParams(
            collective_id=0, has_side_effects=True, vmem_limit_bytes=58 * 1024 * 1024
        ),
    )(
        features,
        projection.T,
        norm_gain.reshape(16, 128),
        norm_shift.reshape(16, 128),
        weight_in,
        weight_out.reshape(weight_out.shape[0], -1),
        cotangent.reshape(cotangent.shape[0], -1),
    )
    mixed, gfeat, gain, shift, gwin, gwout = pl.pallas_call(
        store,
        out_shape=tuple(jax.ShapeDtypeStruct(a.shape, a.dtype) for a in results),
        in_specs=[pl.BlockSpec(memory_space=pl.ANY)] * 6,
        out_specs=(hbm,) * 6,
        scratch_shapes=[pltpu.VMEM(a.shape, a.dtype) for a in results]
        + [pltpu.SemaphoreType.DMA((15,)), pltpu.SemaphoreType.DMA((15,))],
        compiler_params=pltpu.CompilerParams(vmem_limit_bytes=58 * 1024 * 1024),
    )(*results)
    return (
        mixed.reshape(cotangent.shape),
        gfeat,
        gain.reshape(-1),
        shift.reshape(-1),
        gwin,
        gwout.reshape(weight_out.shape),
    )


def solution(mesh):
    placed = (
        P("row", None, "col"),
        P(),
        P(),
        P(),
        P(None, "col"),
        P("col", None, None),
        P("row", None, "col"),
    )
    return jax.shard_map(
        on_device,
        mesh=mesh,
        in_specs=placed,
        out_specs=(
            P("row", None, "col"),
            P("row", None, "col"),
            P(),
            P(),
            P(None, "col"),
            P("col", None, None),
        ),
        check_vma=False,
    )
```

```python
import jax
import jax.numpy as jnp
from jax import lax
from jax.experimental import pallas as pl
from jax.experimental.pallas import tpu as pltpu
from jax.sharding import PartitionSpec as P

MESH = pl.DeviceIdType.MESH
F32 = jnp.float32
BF16 = jnp.bfloat16
NT = (((1,), (1,)), ((), ()))
TN = (((0,), (0,)), ((), ()))


def mm(a, b, dims=(((1,), (0,)), ((), ()))):
    return lax.dot_general(a, b, dims, preferred_element_type=F32)


class Links:
    def __init__(self, send_sems, recv_sems):
        self.send_sems = send_sems
        self.recv_sems = recv_sems
        self.count = 0
        self.sends = []

    def start(self, src, dst, land, row, col):
        i = self.count
        self.count += 1

        def copy(a, b):
            return pltpu.make_async_remote_copy(
                src_ref=a,
                dst_ref=b,
                send_sem=self.send_sems.at[i],
                recv_sem=self.recv_sems.at[i],
                device_id={"row": row, "col": col},
                device_id_type=MESH,
            )

        out = copy(src, dst)
        out.start()
        self.sends.append(out)
        return copy(land, land)

    def flush(self):
        for copy in self.sends:
            copy.wait_send()
        self.sends = []


class Gather:
    def __init__(self, links, buf, where):
        self.links = links
        self.buf = buf
        self.x, self.y, self.zl, self.core, self.row, self.col = where
        self.first = {}
        self.second = {}
        self.sibling = []

    def pos(self, core, df, ds):
        f = (1 - core) * self.x + core * self.y
        s = (1 - core) * self.y + core * self.x
        f = lax.rem(f + df + 4, 4)
        s = lax.rem(s + ds + 4, 4)
        return (1 - core) * (s * 4 + f) + core * (f * 4 + s)

    def block(self, df, ds, zl=None, core=None):
        core = self.core if core is None else core
        p = self.pos(core, df, ds) * 32
        if zl is None:
            return self.buf.at[core, pl.ds(pl.multiple_of(p, 32), 32), :]
        return self.buf.at[core, pl.ds(pl.multiple_of(p + zl * 16, 16), 16), :]

    def start_first(self, diagonal):
        mine = self.block(0, 0, self.zl)
        for df, other in ((0, 1), (1, 0), (-1, 0), (2, 0)) + (((1, 1), (-1, 1), (2, 1)) if diagonal else ()):
            zl = self.zl + other * (1 - 2 * self.zl)
            to = zl * 16 + self.pos(self.core, df, 0)
            self.first[df, other] = self.links.start(
                mine, mine, self.block(-df if df != 2 else 2, 0, zl), to, self.col
            )

    def relay_mate(self):
        self.first.pop((0, 1)).wait_recv()
        zl = 1 - self.zl
        mates = self.block(0, 0, zl)
        for df in (1, -1, 2):
            to = self.zl * 16 + self.pos(self.core, df, 0)
            self.first[df, 1] = self.links.start(
                mates, mates, self.block(-df if df != 2 else 2, 0, zl), to, self.col
            )

    def to_sibling(self, df, ds, zl=None):
        mine = self.block(df, ds, zl)
        self.sibling.append(
            self.links.start(
                mine,
                mine,
                self.block(df, ds, zl, core=1 - self.core),
                self.row,
                self.col + 1 - 2 * self.core,
            )
        )

    def start_second(self, df):
        back = -df if df != 2 else 2
        for other in (0, 1):
            if (back, other) in self.first:
                self.first.pop((back, other)).wait_recv()
        mine = self.block(df, 0)
        for ds in (1, -1, 2):
            to = self.zl * 16 + self.pos(self.core, 0, ds)
            self.second[df, ds] = self.links.start(
                mine, mine, self.block(df, -ds if ds != 2 else 2), to, self.col
            )
        self.to_sibling(df, 0, None if df else 1 - self.zl)

    def end_second(self, df):
        for ds in (1, -1, 2):
            self.second[df, ds].wait_recv()
            self.to_sibling(df, -ds if ds != 2 else 2)

    def end(self):
        for copy in self.sibling:
            copy.wait_recv()


def rows_of(count, width):
    return lax.broadcasted_iota(jnp.int32, (count, width), 0)


def step(
    feat_hbm, proj_hbm, gain_hbm, shift_hbm, win_hbm, wout_hbm, cot_hbm,
    mixed_hbm, gfeat_hbm, gain_out_hbm, shift_out_hbm, gwin_hbm, gwout_hbm,
    feat_ref, proj_ref, norm_ref, win_ref, wout_ref, wink_ref, rows_ref, cots_ref, perm_ref,
    part_ref, half_ref, send_ref, got_ref, inter_ref, unit_ref,
    dpart_ref, dhalf_ref, dsend_ref, dgot_ref, dinter_ref,
    out_ref, got_out_ref, terms_ref, term_half_ref, term_z_ref, term_x_ref, term_y_ref, term_all_ref,
    act_ref, dpre_ref, dact_ref, gfeat_ref, gwin_ref, gwout_ref, mixed_ref, gain_out_ref, shift_out_ref,
    send_sems, recv_sems, local_sems, store_sems,
):
    row = lax.axis_index("row")
    col = lax.axis_index("col")
    x = lax.rem(row, 4)
    y = lax.rem(row // 4, 4)
    zl = row // 16
    core = lax.rem(col, 2)
    sibling = col + 1 - 2 * core
    mine = core * 4
    other = 4 - mine
    peers = [lax.rem(col + k, 8) for k in range(1, 8)]
    sources = [lax.rem(col + 8 - k, 8) for k in range(1, 8)]
    xs = [y * 4 + lax.rem(x + k, 4) for k in range(1, 4)]
    ys = [lax.rem(y + k, 4) * 4 + x for k in range(1, 4)]
    place = y * 4 + x
    mate = (1 - zl) * 16 + place

    barrier = pltpu.get_barrier_semaphore()

    def greet(to_row, to_col):
        pl.semaphore_signal(barrier, inc=1, device_id={"row": to_row, "col": to_col}, device_id_type=MESH)

    here = pl.ds(pl.multiple_of(place * 32 + zl * 16, 16), 16)

    def cot_place(c):
        return cots_ref.at[c // 4, here, pl.ds(pl.multiple_of(lax.rem(c, 4) * 128, 128), 128)]

    loads = [
        pltpu.make_async_copy(feat_hbm.at[pl.ds(4 * i, 4)], feat_ref.at[pl.ds(4 * i, 4)], local_sems.at[i])
        for i in range(4)
    ]
    loads.append(pltpu.make_async_copy(cot_hbm, cot_place(col), local_sems.at[4]))
    loads.append(pltpu.make_async_copy(win_hbm, win_ref, local_sems.at[5]))
    loads.append(pltpu.make_async_copy(wout_hbm, wout_ref, local_sems.at[6]))
    loads.append(pltpu.make_async_copy(gain_hbm, norm_ref.at[0], local_sems.at[7]))
    loads.append(pltpu.make_async_copy(shift_hbm, norm_ref.at[1], local_sems.at[8]))
    load_proj = pltpu.make_async_copy(proj_hbm, proj_ref, local_sems.at[9])
    load_proj.start()
    for copy in loads[:5]:
        copy.start()

    for peer in peers:
        greet(row, peer)
    for p in xs + ys:
        greet(zl * 16 + p, col)
    firsts = [(1 - core) * a + core * b for a, b in zip(xs, ys)]
    for p in firsts:
        greet((1 - zl) * 16 + p, col)
    greet(mate, col)
    for k in (1, 3, 5):
        greet(mate, peers[k])

    batch = rows_of(64, 512) & 15
    batch_d = rows_of(64, 128) & 15
    pick = (rows_of(64, 4) >> 4 == lax.broadcasted_iota(jnp.int32, (64, 4), 1)).astype(F32).astype(BF16)
    load_proj.wait()
    proj = mm(pick, proj_ref[...])
    r = rows_of(512, 512)
    perm_ref[...] = (
        (lax.broadcasted_iota(jnp.int32, (512, 512), 1) == (r & 127) * 4 + (r >> 7)).astype(F32).astype(BF16)
    )

    def pair(q):
        return jnp.concatenate([feat_ref[2 * q], feat_ref[2 * q + 1]], axis=1)

    def by_features(left):
        total = jnp.zeros((64, 256), F32)
        for q in range(8):
            total = total + mm(jnp.where(batch >> 1 == q, left, 0.0).astype(BF16), pair(q))
        return jnp.where(batch_d & 1 == 0, total[:, :128], total[:, 128:])

    def spread(value, q):
        return jnp.concatenate(
            [jnp.where(batch_d == 2 * q + i, value, 0.0) for i in range(2)], axis=1
        ).astype(BF16)

    for copy in loads[:4]:
        copy.wait()
    for copy in loads[5:]:
        copy.start()
    reduced = by_features(proj).astype(BF16).astype(F32)
    inter = jnp.zeros((64, 512), F32)
    for q in range(8):
        inter = inter + mm(spread(reduced, q), pair(q), NT)
    blocks = [inter[16 * (j // 2) : 16 * (j // 2) + 16, 256 * (j % 2) : 256 * (j % 2) + 256] for j in range(8)]
    total = blocks[0]
    for j in range(1, 8):
        total = total + blocks[j]
    mean = jnp.sum(total, axis=1, keepdims=True) * (1.0 / 2048)
    for j in range(8):
        part_ref[j] = blocks[j] - mean

    pl.semaphore_wait(barrier, 20)
    links = Links(send_sems, recv_sems)
    where = (x, y, zl, core, row, col)
    gather_n = Gather(links, rows_ref, where)
    gather_c = Gather(links, cots_ref, where)

    def fold(parts, landing, sending, landed):
        copy = links.start(parts.at[pl.ds(other, 4)], landing, landing, row, sibling)
        yield
        copy.wait_recv()
        for j in range(4):
            sending[j] = (parts[mine + j] + landing[j]).astype(BF16)
        copies = [links.start(sending, landed.at[k], landed.at[k], row, peers[2 * k + 1]) for k in (1, 0, 2)]
        yield
        for copy in copies:
            copy.wait_recv()

    fold_inter = fold(part_ref, half_ref, send_ref, got_ref)
    next(fold_inter)
    next(fold_inter)
    loads[4].wait()
    slices = [
        links.start(cot_place(col), cot_place(col), cot_place(source), row, peer)
        for peer, source in zip(peers, sources)
    ]

    loads[5].wait()
    for J in range(4):
        moved = mm(perm_ref[...], win_ref[512 * J : 512 * J + 512, :]).astype(BF16)
        for k in range(4):
            wink_ref[k * 512 + J * 128 : k * 512 + J * 128 + 128, :] = moved[k * 128 : k * 128 + 128, :]
    loads[7].wait()
    loads[8].wait()
    lines = jnp.concatenate([norm_ref[0], norm_ref[1]], axis=0)
    take = (rows_of(8, 32) & 3) * 4 + (rows_of(8, 32) >> 2) * 16
    both = jnp.concatenate(
        [
            mm((lax.broadcasted_iota(jnp.int32, (8, 32), 1) == take + i).astype(F32).astype(BF16), lines)
            for i in range(4)
        ],
        axis=1,
    ).astype(BF16)
    moved = mm(both, perm_ref[...], NT)
    gains = []
    shifts = []
    for j in range(8):
        k, h = j // 2, j % 2
        for base, into in ((0, gains), (4, shifts)):
            J = base + 2 * h
            into.append(
                jnp.concatenate([moved[J + i : J + i + 1, 128 * k : 128 * k + 128] for i in range(2)], axis=1)
            )

    for copy in slices:
        copy.wait_recv()
    gather_c.start_first(True)
    loads[6].wait()
    dact = jnp.zeros((16, 512), F32)
    for half in range(2):
        dact = dact + mm(cots_ref[half, here, :], wout_ref[:, half * 512 : (half + 1) * 512], NT)

    next(fold_inter, None)
    for j in range(4):
        inter_ref[mine + j] = (send_ref[j].astype(F32) + got_ref[0, j].astype(F32)) + (
            got_ref[1, j].astype(F32) + got_ref[2, j].astype(F32)
        )
    half = inter_ref.at[pl.ds(mine, 4)]
    copy = links.start(half, half, inter_ref.at[pl.ds(other, 4)], row, sibling)
    copy.wait_recv()

    total = inter_ref[0]
    for j in range(1, 8):
        total = total + inter_ref[j]
    mean = jnp.sum(total, axis=1, keepdims=True) * (1.0 / 2048)
    square = jnp.zeros((16, 256), F32)
    for j in range(8):
        centered = inter_ref[j] - mean
        square = square + centered * centered
    rstd = lax.rsqrt(jnp.sum(square, axis=1, keepdims=True) * (1.0 / 2048) + 1e-05)
    normed = []
    for j in range(8):
        unit = (inter_ref[j] - mean) * rstd
        unit_ref[j] = unit
        normed.append((unit * gains[j] + shifts[j]).astype(BF16))
    stacked = jnp.concatenate(
        [
            jnp.concatenate(
                [normed[2 * k + J // 2][:, 128 * (J % 2) : 128 * (J % 2) + 128] for k in range(4)], axis=1
            )
            for J in range(4)
        ],
        axis=0,
    )
    natural = mm(stacked, perm_ref[...]).astype(BF16)
    for J in range(4):
        rows_ref[J // 2, here, 512 * (J % 2) : 512 * (J % 2) + 512] = natural[16 * J : 16 * J + 16, :]
    gather_n.start_first(False)
    order = (0, 1, -1, 2)

    pre = jnp.zeros((16, 512), F32)
    for j in range(8):
        pre = pre + mm(normed[j], wink_ref[j * 256 : (j + 1) * 256, :])
    sigma = 1.0 / (1.0 + jnp.exp(-pre))
    act = (pre * sigma).astype(BF16)
    dpre = (dact * sigma * (1.0 + pre * (1.0 - sigma))).astype(BF16)
    first = jnp.zeros((16, 256), F32)
    second = jnp.zeros((16, 256), F32)
    gain_terms = []
    shift_terms = []
    scaled = []
    for j in range(8):
        dnormed = mm(dpre, wink_ref[j * 256 : (j + 1) * 256, :], NT)
        gain_terms.append(jnp.sum(dnormed * unit_ref[j], axis=0, keepdims=True))
        shift_terms.append(jnp.sum(dnormed, axis=0, keepdims=True))
        scaled.append(dnormed * gains[j])
        first = first + scaled[j]
        second = second + scaled[j] * unit_ref[j]
    first = jnp.sum(first, axis=1, keepdims=True) * (1.0 / 2048)
    second = jnp.sum(second, axis=1, keepdims=True) * (1.0 / 2048)
    for j in range(8):
        dpart_ref[j] = rstd * (scaled[j] - first - unit_ref[j] * second)
    fold_dinter = fold(dpart_ref, dhalf_ref, dsend_ref, dgot_ref)
    next(fold_dinter)
    for h in range(2):
        terms_ref[h] = jnp.concatenate(gain_terms[4 * h : 4 * h + 4] + shift_terms[4 * h : 4 * h + 4], axis=0)
    term = links.start(terms_ref.at[1 - core], term_half_ref, term_half_ref, row, sibling)
    next(fold_dinter)

    def z_of(r, c):
        return (c // 2) * 2 + r // 16

    term.wait_recv()
    at = z_of(row, col)
    term_z_ref[at] = terms_ref[core] + term_half_ref[...]
    terms = []
    for k in range(4):
        for r in (row, mate):
            if k or r is mate:
                to = lax.rem(col + 2 * k, 8)
                source = lax.rem(col + 8 - 2 * k, 8)
                terms.append(
                    links.start(term_z_ref.at[at], term_z_ref.at[at], term_z_ref.at[z_of(r, source)], r, to)
                )
    gather_n.relay_mate()
    for df in order:
        gather_c.start_second(df)
    for j in range(8):
        out_ref[j] = mm(act, wout_ref[:, j * 128 : (j + 1) * 128])
    for df in order:
        gather_n.start_second(df)
    for term in terms:
        term.wait_recv()
    total = term_z_ref[0]
    for k in range(1, 8):
        total = total + term_z_ref[k]
    term_x_ref[x] = total
    terms = [
        links.start(term_x_ref.at[x], term_x_ref.at[x], term_x_ref.at[lax.rem(x + 4 - k, 4)], zl * 16 + xs[k - 1], col)
        for k in range(1, 4)
    ]
    outs = [
        links.start(out_ref.at[peer], got_out_ref.at[k], got_out_ref.at[k], row, peer)
        for k, peer in enumerate(peers)
    ]
    for df in order:
        gather_c.end_second(df)

    next(fold_dinter, None)
    for j in range(4):
        dinter_ref[mine + j] = (
            (dsend_ref[j].astype(F32) + dgot_ref[0, j].astype(F32))
            + (dgot_ref[1, j].astype(F32) + dgot_ref[2, j].astype(F32))
        ).astype(BF16)
    half = dinter_ref.at[pl.ds(mine, 4)]
    copy = links.start(half, half, dinter_ref.at[pl.ds(other, 4)], row, sibling)
    def dacts(i, carry):
        at = pl.ds(pl.multiple_of(i * 256, 256), 256)
        dact_ref[at, :] = mm(cots_ref[0, at, :], wout_ref[:, :512], NT) + mm(
            cots_ref[1, at, :], wout_ref[:, 512:], NT
        )
        return carry

    gather_c.end()
    lax.fori_loop(0, 2, dacts, 0)
    copy.wait_recv()
    dinter = jnp.concatenate(
        [jnp.concatenate([dinter_ref[2 * k], dinter_ref[2 * k + 1]], axis=1) for k in range(4)], axis=0
    ).astype(F32)
    links.flush()
    dreduced = by_features(dinter)
    stores = []
    left = jnp.transpose(jnp.concatenate([dinter, proj], axis=0)).astype(BF16)
    for q in range(8):
        if q == 2:
            for term in terms:
                term.wait_recv()
            term_y_ref[y] = (term_x_ref[0] + term_x_ref[1]) + (term_x_ref[2] + term_x_ref[3])
            terms = [
                links.start(term_y_ref.at[y], term_y_ref.at[y], term_y_ref.at[lax.rem(y + 4 - k, 4)], zl * 16 + ys[k - 1], col)
                for k in range(1, 4)
            ]
        right = jnp.concatenate([spread(reduced, q), spread(dreduced, q)], axis=0)
        grad = mm(left, right).astype(BF16)
        gfeat_ref[2 * q] = grad[:, :128]
        gfeat_ref[2 * q + 1] = grad[:, 128:]
        if q % 2:
            part = pl.ds(2 * q - 2, 4)
            stores.append(
                pltpu.make_async_copy(gfeat_ref.at[part], gfeat_hbm.at[part], store_sems.at[8 + q // 2])
            )
            stores[-1].start()
            gather_n.end_second(order[q // 2])

    mixed = out_ref[col]
    for k, copy in enumerate(outs):
        copy.wait_recv()
        mixed = mixed + got_out_ref[k]
    mixed_ref[...] = mixed.astype(BF16)
    stores.append(pltpu.make_async_copy(mixed_ref, mixed_hbm, store_sems.at[14]))
    stores[-1].start()

    gather_n.end()


    def hidden(i, carry):
        at = pl.ds(pl.multiple_of(i * 256, 256), 256)
        pre = mm(rows_ref[0, at, :], win_ref[:1024, :]) + mm(rows_ref[1, at, :], win_ref[1024:, :])
        sigma = 1.0 / (1.0 + jnp.exp(-pre))
        act_ref[at, :] = (pre * sigma).astype(BF16)
        dpre_ref[at, :] = (dact_ref[at, :] * sigma * (1.0 + pre * (1.0 - sigma))).astype(BF16)
        return carry

    lax.fori_loop(0, 2, hidden, 0)
    for term in terms:
        term.wait_recv()
    term_all_ref[core] = (term_y_ref[0] + term_y_ref[1]) + (term_y_ref[2] + term_y_ref[3])
    term = links.start(term_all_ref.at[core], term_all_ref.at[core], term_all_ref.at[1 - core], row, sibling)

    def grads_in(i, carry):
        at = pl.ds(pl.multiple_of(i * 256, 256), 256)
        columns = pl.ds(pl.multiple_of(lax.rem(i, 4) * 256, 256), 256)
        gwin_ref[at, :] = mm(rows_ref[i // 4, :, columns], dpre_ref[...], TN).astype(BF16)
        pltpu.make_async_copy(gwin_ref.at[at, :], gwin_hbm.at[at, :], store_sems.at[i]).start()
        return carry

    lax.fori_loop(0, 8, grads_in, 0)
    for i in range(8):
        at = pl.ds(i * 256, 256)
        stores.append(pltpu.make_async_copy(gwin_ref.at[at, :], gwin_hbm.at[at, :], store_sems.at[i]))

    term.wait_recv()
    lines = []
    for J in range(4):
        for base in (0, 4):
            lines.append(
                jnp.concatenate(
                    [
                        term_all_ref[
                            k // 2,
                            base + 2 * (k % 2) + J // 2 : base + 2 * (k % 2) + J // 2 + 1,
                            128 * (J % 2) : 128 * (J % 2) + 128,
                        ]
                        for k in range(4)
                    ],
                    axis=1,
                )
            )
    rest = jnp.concatenate(lines, axis=0)
    total = jnp.zeros((8, 512), F32)
    for _ in range(3):
        piece = rest.astype(BF16)
        rest = rest - piece.astype(F32)
        total = total + mm(piece, perm_ref[...])
    for J in range(4):
        gain_out_ref[:, J * 512 : J * 512 + 512] = total[2 * J : 2 * J + 1, :]
        shift_out_ref[:, J * 512 : J * 512 + 512] = total[2 * J + 1 : 2 * J + 2, :]
    stores.append(pltpu.make_async_copy(gain_out_ref, gain_out_hbm, store_sems.at[15]))
    stores[-1].start()
    stores.append(pltpu.make_async_copy(shift_out_ref, shift_out_hbm, store_sems.at[16]))
    stores[-1].start()
    for half in range(2):
        columns = slice(half * 512, (half + 1) * 512)
        gwout_ref[:, columns] = mm(act_ref[...], cots_ref[half], TN).astype(BF16)
        stores.append(
            pltpu.make_async_copy(gwout_ref.at[:, columns], gwout_hbm.at[:, columns], store_sems.at[12 + half])
        )
        stores[-1].start()
    links.flush()
    for copy in stores:
        copy.wait()


def store(*refs):
    sources, targets, held = refs[:6], refs[6:12], refs[12:18]
    loads, stores = [], []
    for source, target, buf in zip(sources, targets, held):
        rows = source.shape[0]
        parts = 4 if rows * source.shape[-1] > 65536 or len(source.shape) == 3 else 1
        for i in range(parts):
            at = pl.ds(i * (rows // parts), rows // parts)
            n = len(loads)
            loads.append(pltpu.make_async_copy(source.at[at], buf.at[at], refs[18].at[n]))
            stores.append(pltpu.make_async_copy(buf.at[at], target.at[at], refs[19].at[n]))
    for copy in loads:
        copy.start()
    for load, save in zip(loads, stores):
        load.wait()
        save.start()
    for save in stores:
        save.wait()


def on_device(features, projection, norm_gain, norm_shift, weight_in, weight_out, cotangent):
    copies = 130
    hbm = pl.BlockSpec(memory_space=pltpu.HBM)
    results = pl.pallas_call(
        step,
        out_shape=(
            jax.ShapeDtypeStruct((16, 128), BF16),
            jax.ShapeDtypeStruct((16, 512, 128), BF16),
            jax.ShapeDtypeStruct((1, 2048), F32),
            jax.ShapeDtypeStruct((1, 2048), F32),
            jax.ShapeDtypeStruct((2048, 512), BF16),
            jax.ShapeDtypeStruct((512, 1024), BF16),
        ),
        in_specs=[hbm] * 7,
        out_specs=(hbm,) * 6,
        scratch_shapes=[
            pltpu.VMEM((16, 512, 128), BF16),
            pltpu.VMEM((4, 512), BF16),
            pltpu.VMEM((2, 16, 128), BF16),
            pltpu.VMEM((2048, 512), BF16),
            pltpu.VMEM((512, 1024), BF16),
            pltpu.VMEM((2048, 512), BF16),
            pltpu.VMEM((2, 512, 1024), BF16),
            pltpu.VMEM((2, 512, 512), BF16),
            pltpu.VMEM((512, 512), BF16),
            pltpu.VMEM((8, 16, 256), F32),
            pltpu.VMEM((4, 16, 256), F32),
            pltpu.VMEM((4, 16, 256), BF16),
            pltpu.VMEM((3, 4, 16, 256), BF16),
            pltpu.VMEM((8, 16, 256), F32),
            pltpu.VMEM((8, 16, 256), F32),
            pltpu.VMEM((8, 16, 256), F32),
            pltpu.VMEM((4, 16, 256), F32),
            pltpu.VMEM((4, 16, 256), BF16),
            pltpu.VMEM((3, 4, 16, 256), BF16),
            pltpu.VMEM((8, 16, 256), BF16),
            pltpu.VMEM((8, 16, 128), F32),
            pltpu.VMEM((7, 16, 128), F32),
            pltpu.VMEM((2, 8, 256), F32),
            pltpu.VMEM((8, 256), F32),
            pltpu.VMEM((8, 8, 256), F32),
            pltpu.VMEM((4, 8, 256), F32),
            pltpu.VMEM((4, 8, 256), F32),
            pltpu.VMEM((2, 8, 256), F32),
            pltpu.VMEM((512, 512), BF16),
            pltpu.VMEM((512, 512), BF16),
            pltpu.VMEM((512, 512), F32),
            pltpu.VMEM((16, 512, 128), BF16),
            pltpu.VMEM((2048, 512), BF16),
            pltpu.VMEM((512, 1024), BF16),
            pltpu.VMEM((16, 128), BF16),
            pltpu.VMEM((1, 2048), F32),
            pltpu.VMEM((1, 2048), F32),
            pltpu.SemaphoreType.DMA((copies,)),
            pltpu.SemaphoreType.DMA((copies,)),
            pltpu.SemaphoreType.DMA((10,)),
            pltpu.SemaphoreType.DMA((17,)),
        ],
        compiler_params=pltpu.CompilerParams(
            collective_id=0, has_side_effects=True, vmem_limit_bytes=58 * 1024 * 1024
        ),
    )(
        features,
        projection.T,
        norm_gain.reshape(16, 128),
        norm_shift.reshape(16, 128),
        weight_in,
        weight_out.reshape(weight_out.shape[0], -1),
        cotangent.reshape(cotangent.shape[0], -1),
    )
    mixed, gfeat, gain, shift, gwin, gwout = pl.pallas_call(
        store,
        out_shape=tuple(jax.ShapeDtypeStruct(a.shape, a.dtype) for a in results),
        in_specs=[pl.BlockSpec(memory_space=pl.ANY)] * 6,
        out_specs=(hbm,) * 6,
        scratch_shapes=[pltpu.VMEM(a.shape, a.dtype) for a in results]
        + [pltpu.SemaphoreType.DMA((15,)), pltpu.SemaphoreType.DMA((15,))],
        compiler_params=pltpu.CompilerParams(vmem_limit_bytes=58 * 1024 * 1024),
    )(*results)
    return (
        mixed.reshape(cotangent.shape),
        gfeat,
        gain.reshape(-1),
        shift.reshape(-1),
        gwin,
        gwout.reshape(weight_out.shape),
    )


def solution(mesh):
    placed = (
        P("row", None, "col"),
        P(),
        P(),
        P(),
        P(None, "col"),
        P("col", None, None),
        P("row", None, "col"),
    )
    return jax.shard_map(
        on_device,
        mesh=mesh,
        in_specs=placed,
        out_specs=(
            P("row", None, "col"),
            P("row", None, "col"),
            P(),
            P(),
            P(None, "col"),
            P("col", None, None),
        ),
        check_vma=False,
    )
```

```python
import jax
import jax.numpy as jnp
from jax import lax
from jax.experimental import pallas as pl
from jax.experimental.pallas import tpu as pltpu
from jax.sharding import PartitionSpec as P

MESH = pl.DeviceIdType.MESH
F32 = jnp.float32
BF16 = jnp.bfloat16
NT = (((1,), (1,)), ((), ()))
TN = (((0,), (0,)), ((), ()))


def mm(a, b, dims=(((1,), (0,)), ((), ()))):
    return lax.dot_general(a, b, dims, preferred_element_type=F32)


class Links:
    def __init__(self, send_sems, recv_sems):
        self.send_sems = send_sems
        self.recv_sems = recv_sems
        self.count = 0
        self.sends = []

    def start(self, src, dst, land, row, col):
        i = self.count
        self.count += 1

        def copy(a, b):
            return pltpu.make_async_remote_copy(
                src_ref=a,
                dst_ref=b,
                send_sem=self.send_sems.at[i],
                recv_sem=self.recv_sems.at[i],
                device_id={"row": row, "col": col},
                device_id_type=MESH,
            )

        out = copy(src, dst)
        out.start()
        self.sends.append(out)
        return copy(land, land)

    def flush(self):
        for copy in self.sends:
            copy.wait_send()
        self.sends = []


class Gather:
    def __init__(self, links, buf, where):
        self.links = links
        self.buf = buf
        self.x, self.y, self.zl, self.core, self.row, self.col = where
        self.first = {}
        self.second = {}
        self.sibling = []

    def pos(self, core, df, ds):
        f = (1 - core) * self.x + core * self.y
        s = (1 - core) * self.y + core * self.x
        f = lax.rem(f + df + 4, 4)
        s = lax.rem(s + ds + 4, 4)
        return (1 - core) * (s * 4 + f) + core * (f * 4 + s)

    def block(self, df, ds, zl=None, core=None):
        core = self.core if core is None else core
        p = self.pos(core, df, ds) * 32
        if zl is None:
            return self.buf.at[core, pl.ds(pl.multiple_of(p, 32), 32), :]
        return self.buf.at[core, pl.ds(pl.multiple_of(p + zl * 16, 16), 16), :]

    def start_first(self):
        mine = self.block(0, 0, self.zl)
        for df, other in ((0, 1), (1, 0), (-1, 0), (2, 0), (1, 1), (-1, 1), (2, 1)):
            zl = self.zl + other * (1 - 2 * self.zl)
            to = zl * 16 + self.pos(self.core, df, 0)
            self.first[df, other] = self.links.start(
                mine, mine, self.block(-df if df != 2 else 2, 0, zl), to, self.col
            )

    def to_sibling(self, df, ds, zl=None):
        mine = self.block(df, ds, zl)
        self.sibling.append(
            self.links.start(
                mine,
                mine,
                self.block(df, ds, zl, core=1 - self.core),
                self.row,
                self.col + 1 - 2 * self.core,
            )
        )

    def start_second(self, df):
        back = -df if df != 2 else 2
        for other in (0, 1):
            if (back, other) in self.first:
                self.first.pop((back, other)).wait_recv()
        mine = self.block(df, 0)
        for ds in (1, -1, 2):
            to = self.zl * 16 + self.pos(self.core, 0, ds)
            self.second[df, ds] = self.links.start(
                mine, mine, self.block(df, -ds if ds != 2 else 2), to, self.col
            )
        self.to_sibling(df, 0, None if df else 1 - self.zl)

    def end_second(self, df):
        for ds in (1, -1, 2):
            self.second[df, ds].wait_recv()
            self.to_sibling(df, -ds if ds != 2 else 2)

    def end(self):
        for copy in self.sibling:
            copy.wait_recv()


def rows_of(count, width):
    return lax.broadcasted_iota(jnp.int32, (count, width), 0)


def step(
    feat_hbm, proj_hbm, gain_hbm, shift_hbm, win_hbm, wout_hbm, cot_hbm,
    mixed_hbm, gfeat_hbm, gain_out_hbm, shift_out_hbm, gwin_hbm, gwout_hbm,
    feat_ref, proj_ref, norm_ref, win_ref, wout_ref, wink_ref, rows_ref, cots_ref, perm_ref,
    part_ref, half_ref, send_ref, got_ref, inter_ref, unit_ref,
    dpart_ref, dhalf_ref, dsend_ref, dgot_ref, dinter_ref,
    out_ref, got_out_ref, terms_ref, term_half_ref, term_z_ref, term_x_ref, term_y_ref, term_all_ref,
    act_ref, dpre_ref, dact_ref, gfeat_ref, gwin_ref, gwout_ref, mixed_ref, gain_out_ref, shift_out_ref,
    send_sems, recv_sems, local_sems, store_sems,
):
    row = lax.axis_index("row")
    col = lax.axis_index("col")
    x = lax.rem(row, 4)
    y = lax.rem(row // 4, 4)
    zl = row // 16
    core = lax.rem(col, 2)
    sibling = col + 1 - 2 * core
    mine = core * 4
    other = 4 - mine
    peers = [lax.rem(col + k, 8) for k in range(1, 8)]
    sources = [lax.rem(col + 8 - k, 8) for k in range(1, 8)]
    xs = [y * 4 + lax.rem(x + k, 4) for k in range(1, 4)]
    ys = [lax.rem(y + k, 4) * 4 + x for k in range(1, 4)]
    place = y * 4 + x
    mate = (1 - zl) * 16 + place

    barrier = pltpu.get_barrier_semaphore()

    def greet(to_row, to_col):
        pl.semaphore_signal(barrier, inc=1, device_id={"row": to_row, "col": to_col}, device_id_type=MESH)

    here = pl.ds(pl.multiple_of(place * 32 + zl * 16, 16), 16)

    def cot_place(c):
        return cots_ref.at[c // 4, here, pl.ds(pl.multiple_of(lax.rem(c, 4) * 128, 128), 128)]

    loads = [
        pltpu.make_async_copy(feat_hbm.at[pl.ds(4 * i, 4)], feat_ref.at[pl.ds(4 * i, 4)], local_sems.at[i])
        for i in range(4)
    ]
    loads.append(pltpu.make_async_copy(cot_hbm, cot_place(col), local_sems.at[4]))
    loads.append(pltpu.make_async_copy(win_hbm, win_ref, local_sems.at[5]))
    loads.append(pltpu.make_async_copy(wout_hbm, wout_ref, local_sems.at[6]))
    loads.append(pltpu.make_async_copy(gain_hbm, norm_ref.at[0], local_sems.at[7]))
    loads.append(pltpu.make_async_copy(shift_hbm, norm_ref.at[1], local_sems.at[8]))
    load_proj = pltpu.make_async_copy(proj_hbm, proj_ref, local_sems.at[9])
    load_proj.start()
    for copy in loads[:5]:
        copy.start()

    for peer in peers:
        greet(row, peer)
    for p in xs + ys:
        greet(zl * 16 + p, col)
    firsts = [(1 - core) * a + core * b for a, b in zip(xs, ys)]
    for p in firsts:
        greet((1 - zl) * 16 + p, col)
    greet(mate, col)
    for k in (1, 3, 5):
        greet(mate, peers[k])

    batch = rows_of(64, 512) & 15
    batch_d = rows_of(64, 128) & 15
    pick = (rows_of(64, 4) >> 4 == lax.broadcasted_iota(jnp.int32, (64, 4), 1)).astype(F32).astype(BF16)
    load_proj.wait()
    proj = mm(pick, proj_ref[...])
    r = rows_of(512, 512)
    perm_ref[...] = (
        (lax.broadcasted_iota(jnp.int32, (512, 512), 1) == (r & 127) * 4 + (r >> 7)).astype(F32).astype(BF16)
    )

    def pair(q):
        return jnp.concatenate([feat_ref[2 * q], feat_ref[2 * q + 1]], axis=1)

    def by_features(left):
        total = jnp.zeros((64, 256), F32)
        for q in range(8):
            total = total + mm(jnp.where(batch >> 1 == q, left, 0.0).astype(BF16), pair(q))
        return jnp.where(batch_d & 1 == 0, total[:, :128], total[:, 128:])

    def spread(value, q):
        return jnp.concatenate(
            [jnp.where(batch_d == 2 * q + i, value, 0.0) for i in range(2)], axis=1
        ).astype(BF16)

    for copy in loads[:4]:
        copy.wait()
    for copy in loads[5:]:
        copy.start()
    reduced = by_features(proj).astype(BF16).astype(F32)
    inter = jnp.zeros((64, 512), F32)
    for q in range(8):
        inter = inter + mm(spread(reduced, q), pair(q), NT)
    blocks = [inter[16 * (j // 2) : 16 * (j // 2) + 16, 256 * (j % 2) : 256 * (j % 2) + 256] for j in range(8)]
    total = blocks[0]
    for j in range(1, 8):
        total = total + blocks[j]
    mean = jnp.sum(total, axis=1, keepdims=True) * (1.0 / 2048)
    for j in range(8):
        part_ref[j] = blocks[j] - mean

    pl.semaphore_wait(barrier, 20)
    links = Links(send_sems, recv_sems)
    where = (x, y, zl, core, row, col)
    gather_n = Gather(links, rows_ref, where)
    gather_c = Gather(links, cots_ref, where)

    def fold(parts, landing, sending, landed):
        copy = links.start(parts.at[pl.ds(other, 4)], landing, landing, row, sibling)
        yield
        copy.wait_recv()
        for j in range(4):
            sending[j] = (parts[mine + j] + landing[j]).astype(BF16)
        copies = [links.start(sending, landed.at[k], landed.at[k], row, peers[2 * k + 1]) for k in (1, 0, 2)]
        yield
        for copy in copies:
            copy.wait_recv()

    fold_inter = fold(part_ref, half_ref, send_ref, got_ref)
    next(fold_inter)
    next(fold_inter)
    loads[4].wait()
    slices = [
        links.start(cot_place(col), cot_place(col), cot_place(source), row, peer)
        for peer, source in zip(peers, sources)
    ]

    loads[5].wait()
    for J in range(4):
        moved = mm(perm_ref[...], win_ref[512 * J : 512 * J + 512, :]).astype(BF16)
        for k in range(4):
            wink_ref[k * 512 + J * 128 : k * 512 + J * 128 + 128, :] = moved[k * 128 : k * 128 + 128, :]
    loads[7].wait()
    loads[8].wait()
    lines = jnp.concatenate([norm_ref[0], norm_ref[1]], axis=0)
    take = (rows_of(8, 32) & 3) * 4 + (rows_of(8, 32) >> 2) * 16
    both = jnp.concatenate(
        [
            mm((lax.broadcasted_iota(jnp.int32, (8, 32), 1) == take + i).astype(F32).astype(BF16), lines)
            for i in range(4)
        ],
        axis=1,
    ).astype(BF16)
    moved = mm(both, perm_ref[...], NT)
    gains = []
    shifts = []
    for j in range(8):
        k, h = j // 2, j % 2
        for base, into in ((0, gains), (4, shifts)):
            J = base + 2 * h
            into.append(
                jnp.concatenate([moved[J + i : J + i + 1, 128 * k : 128 * k + 128] for i in range(2)], axis=1)
            )

    for copy in slices:
        copy.wait_recv()
    gather_c.start_first()
    loads[6].wait()
    dact = jnp.zeros((16, 512), F32)
    for half in range(2):
        dact = dact + mm(cots_ref[half, here, :], wout_ref[:, half * 512 : (half + 1) * 512], NT)

    next(fold_inter, None)
    for j in range(4):
        inter_ref[mine + j] = (send_ref[j].astype(F32) + got_ref[0, j].astype(F32)) + (
            got_ref[1, j].astype(F32) + got_ref[2, j].astype(F32)
        )
    half = inter_ref.at[pl.ds(mine, 4)]
    copy = links.start(half, half, inter_ref.at[pl.ds(other, 4)], row, sibling)
    copy.wait_recv()

    total = inter_ref[0]
    for j in range(1, 8):
        total = total + inter_ref[j]
    mean = jnp.sum(total, axis=1, keepdims=True) * (1.0 / 2048)
    square = jnp.zeros((16, 256), F32)
    for j in range(8):
        centered = inter_ref[j] - mean
        square = square + centered * centered
    rstd = lax.rsqrt(jnp.sum(square, axis=1, keepdims=True) * (1.0 / 2048) + 1e-05)
    normed = []
    for j in range(8):
        unit = (inter_ref[j] - mean) * rstd
        unit_ref[j] = unit
        normed.append((unit * gains[j] + shifts[j]).astype(BF16))
    stacked = jnp.concatenate(
        [
            jnp.concatenate(
                [normed[2 * k + J // 2][:, 128 * (J % 2) : 128 * (J % 2) + 128] for k in range(4)], axis=1
            )
            for J in range(4)
        ],
        axis=0,
    )
    natural = mm(stacked, perm_ref[...]).astype(BF16)
    for J in range(4):
        rows_ref[J // 2, here, 512 * (J % 2) : 512 * (J % 2) + 512] = natural[16 * J : 16 * J + 16, :]
    gather_n.start_first()
    order = (0, 1, -1, 2)

    pre = jnp.zeros((16, 512), F32)
    for j in range(8):
        pre = pre + mm(normed[j], wink_ref[j * 256 : (j + 1) * 256, :])
    sigma = 1.0 / (1.0 + jnp.exp(-pre))
    act = (pre * sigma).astype(BF16)
    dpre = (dact * sigma * (1.0 + pre * (1.0 - sigma))).astype(BF16)
    first = jnp.zeros((16, 256), F32)
    second = jnp.zeros((16, 256), F32)
    gain_terms = []
    shift_terms = []
    scaled = []
    for j in range(8):
        dnormed = mm(dpre, wink_ref[j * 256 : (j + 1) * 256, :], NT)
        gain_terms.append(jnp.sum(dnormed * unit_ref[j], axis=0, keepdims=True))
        shift_terms.append(jnp.sum(dnormed, axis=0, keepdims=True))
        scaled.append(dnormed * gains[j])
        first = first + scaled[j]
        second = second + scaled[j] * unit_ref[j]
    first = jnp.sum(first, axis=1, keepdims=True) * (1.0 / 2048)
    second = jnp.sum(second, axis=1, keepdims=True) * (1.0 / 2048)
    for j in range(8):
        dpart_ref[j] = rstd * (scaled[j] - first - unit_ref[j] * second)
    fold_dinter = fold(dpart_ref, dhalf_ref, dsend_ref, dgot_ref)
    next(fold_dinter)
    for df in order:
        gather_c.start_second(df)
    for h in range(2):
        terms_ref[h] = jnp.concatenate(gain_terms[4 * h : 4 * h + 4] + shift_terms[4 * h : 4 * h + 4], axis=0)
    term = links.start(terms_ref.at[1 - core], term_half_ref, term_half_ref, row, sibling)
    next(fold_dinter)

    def z_of(r, c):
        return (c // 2) * 2 + r // 16

    term.wait_recv()
    at = z_of(row, col)
    term_z_ref[at] = terms_ref[core] + term_half_ref[...]
    terms = []
    for k in range(4):
        for r in (row, mate):
            if k or r is mate:
                to = lax.rem(col + 2 * k, 8)
                source = lax.rem(col + 8 - 2 * k, 8)
                terms.append(
                    links.start(term_z_ref.at[at], term_z_ref.at[at], term_z_ref.at[z_of(r, source)], r, to)
                )
    for j in range(8):
        out_ref[j] = mm(act, wout_ref[:, j * 128 : (j + 1) * 128])
    for df in order:
        gather_n.start_second(df)
    for term in terms:
        term.wait_recv()
    total = term_z_ref[0]
    for k in range(1, 8):
        total = total + term_z_ref[k]
    term_x_ref[x] = total
    terms = [
        links.start(term_x_ref.at[x], term_x_ref.at[x], term_x_ref.at[lax.rem(x + 4 - k, 4)], zl * 16 + xs[k - 1], col)
        for k in range(1, 4)
    ]
    outs = [
        links.start(out_ref.at[peer], got_out_ref.at[k], got_out_ref.at[k], row, peer)
        for k, peer in enumerate(peers)
    ]
    for df in order:
        gather_c.end_second(df)

    next(fold_dinter, None)
    for j in range(4):
        dinter_ref[mine + j] = (
            (dsend_ref[j].astype(F32) + dgot_ref[0, j].astype(F32))
            + (dgot_ref[1, j].astype(F32) + dgot_ref[2, j].astype(F32))
        ).astype(BF16)
    half = dinter_ref.at[pl.ds(mine, 4)]
    copy = links.start(half, half, dinter_ref.at[pl.ds(other, 4)], row, sibling)
    def dacts(i, carry):
        at = pl.ds(pl.multiple_of(i * 256, 256), 256)
        dact_ref[at, :] = mm(cots_ref[0, at, :], wout_ref[:, :512], NT) + mm(
            cots_ref[1, at, :], wout_ref[:, 512:], NT
        )
        return carry

    gather_c.end()
    lax.fori_loop(0, 2, dacts, 0)
    copy.wait_recv()
    dinter = jnp.concatenate(
        [jnp.concatenate([dinter_ref[2 * k], dinter_ref[2 * k + 1]], axis=1) for k in range(4)], axis=0
    ).astype(F32)
    links.flush()
    dreduced = by_features(dinter)
    stores = []
    left = jnp.transpose(jnp.concatenate([dinter, proj], axis=0)).astype(BF16)
    for q in range(8):
        if q == 2:
            for term in terms:
                term.wait_recv()
            term_y_ref[y] = (term_x_ref[0] + term_x_ref[1]) + (term_x_ref[2] + term_x_ref[3])
            terms = [
                links.start(term_y_ref.at[y], term_y_ref.at[y], term_y_ref.at[lax.rem(y + 4 - k, 4)], zl * 16 + ys[k - 1], col)
                for k in range(1, 4)
            ]
        right = jnp.concatenate([spread(reduced, q), spread(dreduced, q)], axis=0)
        grad = mm(left, right).astype(BF16)
        gfeat_ref[2 * q] = grad[:, :128]
        gfeat_ref[2 * q + 1] = grad[:, 128:]
        if q % 2:
            part = pl.ds(2 * q - 2, 4)
            stores.append(
                pltpu.make_async_copy(gfeat_ref.at[part], gfeat_hbm.at[part], store_sems.at[8 + q // 2])
            )
            stores[-1].start()
            gather_n.end_second(order[q // 2])

    mixed = out_ref[col]
    for k, copy in enumerate(outs):
        copy.wait_recv()
        mixed = mixed + got_out_ref[k]
    mixed_ref[...] = mixed.astype(BF16)
    stores.append(pltpu.make_async_copy(mixed_ref, mixed_hbm, store_sems.at[14]))
    stores[-1].start()

    gather_n.end()


    def hidden(i, carry):
        at = pl.ds(pl.multiple_of(i * 256, 256), 256)
        pre = mm(rows_ref[0, at, :], win_ref[:1024, :]) + mm(rows_ref[1, at, :], win_ref[1024:, :])
        sigma = 1.0 / (1.0 + jnp.exp(-pre))
        act_ref[at, :] = (pre * sigma).astype(BF16)
        dpre_ref[at, :] = (dact_ref[at, :] * sigma * (1.0 + pre * (1.0 - sigma))).astype(BF16)
        return carry

    lax.fori_loop(0, 2, hidden, 0)
    for term in terms:
        term.wait_recv()
    term_all_ref[core] = (term_y_ref[0] + term_y_ref[1]) + (term_y_ref[2] + term_y_ref[3])
    term = links.start(term_all_ref.at[core], term_all_ref.at[core], term_all_ref.at[1 - core], row, sibling)

    def grads_in(i, carry):
        at = pl.ds(pl.multiple_of(i * 256, 256), 256)
        columns = pl.ds(pl.multiple_of(lax.rem(i, 4) * 256, 256), 256)
        gwin_ref[at, :] = mm(rows_ref[i // 4, :, columns], dpre_ref[...], TN).astype(BF16)
        pltpu.make_async_copy(gwin_ref.at[at, :], gwin_hbm.at[at, :], store_sems.at[i]).start()
        return carry

    lax.fori_loop(0, 8, grads_in, 0)
    for i in range(8):
        at = pl.ds(i * 256, 256)
        stores.append(pltpu.make_async_copy(gwin_ref.at[at, :], gwin_hbm.at[at, :], store_sems.at[i]))

    term.wait_recv()
    lines = []
    for J in range(4):
        for base in (0, 4):
            lines.append(
                jnp.concatenate(
                    [
                        term_all_ref[
                            k // 2,
                            base + 2 * (k % 2) + J // 2 : base + 2 * (k % 2) + J // 2 + 1,
                            128 * (J % 2) : 128 * (J % 2) + 128,
                        ]
                        for k in range(4)
                    ],
                    axis=1,
                )
            )
    rest = jnp.concatenate(lines, axis=0)
    total = jnp.zeros((8, 512), F32)
    for _ in range(3):
        piece = rest.astype(BF16)
        rest = rest - piece.astype(F32)
        total = total + mm(piece, perm_ref[...])
    for J in range(4):
        gain_out_ref[:, J * 512 : J * 512 + 512] = total[2 * J : 2 * J + 1, :]
        shift_out_ref[:, J * 512 : J * 512 + 512] = total[2 * J + 1 : 2 * J + 2, :]
    stores.append(pltpu.make_async_copy(gain_out_ref, gain_out_hbm, store_sems.at[15]))
    stores[-1].start()
    stores.append(pltpu.make_async_copy(shift_out_ref, shift_out_hbm, store_sems.at[16]))
    stores[-1].start()
    for half in range(2):
        columns = slice(half * 512, (half + 1) * 512)
        gwout_ref[:, columns] = mm(act_ref[...], cots_ref[half], TN).astype(BF16)
        stores.append(
            pltpu.make_async_copy(gwout_ref.at[:, columns], gwout_hbm.at[:, columns], store_sems.at[12 + half])
        )
        stores[-1].start()
    links.flush()
    for copy in stores:
        copy.wait()


def store(*refs):
    loads = [pltpu.make_async_copy(refs[i], refs[12 + i], refs[18].at[i]) for i in range(6)]
    saves = [pltpu.make_async_copy(refs[12 + i], refs[6 + i], refs[19].at[i]) for i in range(6)]
    for copy in loads:
        copy.start()
    for load, save in zip(loads, saves):
        load.wait()
        save.start()
    for save in saves:
        save.wait()


def on_device(features, projection, norm_gain, norm_shift, weight_in, weight_out, cotangent):
    copies = 130
    hbm = pl.BlockSpec(memory_space=pltpu.HBM)
    results = pl.pallas_call(
        step,
        out_shape=(
            jax.ShapeDtypeStruct((16, 128), BF16),
            jax.ShapeDtypeStruct((16, 512, 128), BF16),
            jax.ShapeDtypeStruct((1, 2048), F32),
            jax.ShapeDtypeStruct((1, 2048), F32),
            jax.ShapeDtypeStruct((2048, 512), BF16),
            jax.ShapeDtypeStruct((512, 1024), BF16),
        ),
        in_specs=[hbm] * 7,
        out_specs=(hbm,) * 6,
        scratch_shapes=[
            pltpu.VMEM((16, 512, 128), BF16),
            pltpu.VMEM((4, 512), BF16),
            pltpu.VMEM((2, 16, 128), BF16),
            pltpu.VMEM((2048, 512), BF16),
            pltpu.VMEM((512, 1024), BF16),
            pltpu.VMEM((2048, 512), BF16),
            pltpu.VMEM((2, 512, 1024), BF16),
            pltpu.VMEM((2, 512, 512), BF16),
            pltpu.VMEM((512, 512), BF16),
            pltpu.VMEM((8, 16, 256), F32),
            pltpu.VMEM((4, 16, 256), F32),
            pltpu.VMEM((4, 16, 256), BF16),
            pltpu.VMEM((3, 4, 16, 256), BF16),
            pltpu.VMEM((8, 16, 256), F32),
            pltpu.VMEM((8, 16, 256), F32),
            pltpu.VMEM((8, 16, 256), F32),
            pltpu.VMEM((4, 16, 256), F32),
            pltpu.VMEM((4, 16, 256), BF16),
            pltpu.VMEM((3, 4, 16, 256), BF16),
            pltpu.VMEM((8, 16, 256), BF16),
            pltpu.VMEM((8, 16, 128), F32),
            pltpu.VMEM((7, 16, 128), F32),
            pltpu.VMEM((2, 8, 256), F32),
            pltpu.VMEM((8, 256), F32),
            pltpu.VMEM((8, 8, 256), F32),
            pltpu.VMEM((4, 8, 256), F32),
            pltpu.VMEM((4, 8, 256), F32),
            pltpu.VMEM((2, 8, 256), F32),
            pltpu.VMEM((512, 512), BF16),
            pltpu.VMEM((512, 512), BF16),
            pltpu.VMEM((512, 512), F32),
            pltpu.VMEM((16, 512, 128), BF16),
            pltpu.VMEM((2048, 512), BF16),
            pltpu.VMEM((512, 1024), BF16),
            pltpu.VMEM((16, 128), BF16),
            pltpu.VMEM((1, 2048), F32),
            pltpu.VMEM((1, 2048), F32),
            pltpu.SemaphoreType.DMA((copies,)),
            pltpu.SemaphoreType.DMA((copies,)),
            pltpu.SemaphoreType.DMA((10,)),
            pltpu.SemaphoreType.DMA((17,)),
        ],
        compiler_params=pltpu.CompilerParams(
            collective_id=0, has_side_effects=True, vmem_limit_bytes=58 * 1024 * 1024
        ),
    )(
        features,
        projection.T,
        norm_gain.reshape(16, 128),
        norm_shift.reshape(16, 128),
        weight_in,
        weight_out.reshape(weight_out.shape[0], -1),
        cotangent.reshape(cotangent.shape[0], -1),
    )
    mixed, gfeat, gain, shift, gwin, gwout = pl.pallas_call(
        store,
        out_shape=tuple(jax.ShapeDtypeStruct(a.shape, a.dtype) for a in results),
        in_specs=[pl.BlockSpec(memory_space=pl.ANY)] * 6,
        out_specs=(hbm,) * 6,
        scratch_shapes=[pltpu.VMEM(a.shape, a.dtype) for a in results]
        + [pltpu.SemaphoreType.DMA((6,)), pltpu.SemaphoreType.DMA((6,))],
        compiler_params=pltpu.CompilerParams(vmem_limit_bytes=58 * 1024 * 1024),
    )(*results)
    return (
        mixed.reshape(cotangent.shape),
        gfeat,
        gain.reshape(-1),
        shift.reshape(-1),
        gwin,
        gwout.reshape(weight_out.shape),
    )


def solution(mesh):
    placed = (
        P("row", None, "col"),
        P(),
        P(),
        P(),
        P(None, "col"),
        P("col", None, None),
        P("row", None, "col"),
    )
    return jax.shard_map(
        on_device,
        mesh=mesh,
        in_specs=placed,
        out_specs=(
            P("row", None, "col"),
            P("row", None, "col"),
            P(),
            P(),
            P(None, "col"),
            P("col", None, None),
        ),
        check_vma=False,
    )
```

```python
import jax
import jax.numpy as jnp
from jax import lax
from jax.experimental import pallas as pl
from jax.experimental.pallas import tpu as pltpu
from jax.sharding import PartitionSpec as P

MESH = pl.DeviceIdType.MESH
F32 = jnp.float32
BF16 = jnp.bfloat16
NT = (((1,), (1,)), ((), ()))
TN = (((0,), (0,)), ((), ()))


def mm(a, b, dims=(((1,), (0,)), ((), ()))):
    return lax.dot_general(a, b, dims, preferred_element_type=F32)


class Links:
    def __init__(self, send_sems, recv_sems):
        self.send_sems = send_sems
        self.recv_sems = recv_sems
        self.count = 0
        self.sends = []

    def start(self, src, dst, land, row, col):
        i = self.count
        self.count += 1

        def copy(a, b):
            return pltpu.make_async_remote_copy(
                src_ref=a,
                dst_ref=b,
                send_sem=self.send_sems.at[i],
                recv_sem=self.recv_sems.at[i],
                device_id={"row": row, "col": col},
                device_id_type=MESH,
            )

        out = copy(src, dst)
        out.start()
        self.sends.append(out)
        return copy(land, land)

    def flush(self):
        for copy in self.sends:
            copy.wait_send()
        self.sends = []


class Gather:
    def __init__(self, links, buf, where):
        self.links = links
        self.buf = buf
        self.x, self.y, self.zl, self.core, self.row, self.col = where
        self.first = {}
        self.second = {}
        self.sibling = []

    def pos(self, core, df, ds):
        f = (1 - core) * self.x + core * self.y
        s = (1 - core) * self.y + core * self.x
        f = lax.rem(f + df + 4, 4)
        s = lax.rem(s + ds + 4, 4)
        return (1 - core) * (s * 4 + f) + core * (f * 4 + s)

    def block(self, df, ds, zl=None, core=None):
        core = self.core if core is None else core
        p = self.pos(core, df, ds) * 32
        if zl is None:
            return self.buf.at[core, pl.ds(pl.multiple_of(p, 32), 32), :]
        return self.buf.at[core, pl.ds(pl.multiple_of(p + zl * 16, 16), 16), :]

    def start_first(self):
        mine = self.block(0, 0, self.zl)
        for df, other in ((0, 1), (1, 0), (-1, 0), (2, 0), (1, 1), (-1, 1), (2, 1)):
            zl = self.zl + other * (1 - 2 * self.zl)
            to = zl * 16 + self.pos(self.core, df, 0)
            self.first[df, other] = self.links.start(
                mine, mine, self.block(-df if df != 2 else 2, 0, zl), to, self.col
            )

    def to_sibling(self, df, ds, zl=None):
        mine = self.block(df, ds, zl)
        self.sibling.append(
            self.links.start(
                mine,
                mine,
                self.block(df, ds, zl, core=1 - self.core),
                self.row,
                self.col + 1 - 2 * self.core,
            )
        )

    def start_second(self, df):
        back = -df if df != 2 else 2
        for other in (0, 1):
            if (back, other) in self.first:
                self.first.pop((back, other)).wait_recv()
        mine = self.block(df, 0)
        for ds in (1, -1, 2):
            to = self.zl * 16 + self.pos(self.core, 0, ds)
            self.second[df, ds] = self.links.start(
                mine, mine, self.block(df, -ds if ds != 2 else 2), to, self.col
            )
        self.to_sibling(df, 0, None if df else 1 - self.zl)

    def end_second(self, df):
        for ds in (1, -1, 2):
            self.second[df, ds].wait_recv()
            self.to_sibling(df, -ds if ds != 2 else 2)

    def end(self):
        for copy in self.sibling:
            copy.wait_recv()


def rows_of(count, width):
    return lax.broadcasted_iota(jnp.int32, (count, width), 0)


def step(
    feat_hbm, proj_hbm, gain_hbm, shift_hbm, win_hbm, wout_hbm, cot_hbm,
    mixed_hbm, gfeat_hbm, gain_out_hbm, shift_out_hbm, gwin_hbm, gwout_hbm,
    feat_ref, proj_ref, norm_ref, win_ref, wout_ref, wink_ref, rows_ref, cots_ref, perm_ref,
    part_ref, half_ref, send_ref, got_ref, inter_ref, unit_ref,
    dpart_ref, dhalf_ref, dsend_ref, dgot_ref, dinter_ref,
    out_ref, got_out_ref, terms_ref, term_half_ref, term_z_ref, term_x_ref, term_y_ref, term_all_ref,
    act_ref, dpre_ref, dact_ref, gfeat_ref, gwin_ref, gwout_ref, mixed_ref, gain_out_ref, shift_out_ref,
    send_sems, recv_sems, local_sems, store_sems,
):
    row = lax.axis_index("row")
    col = lax.axis_index("col")
    x = lax.rem(row, 4)
    y = lax.rem(row // 4, 4)
    zl = row // 16
    core = lax.rem(col, 2)
    sibling = col + 1 - 2 * core
    mine = core * 4
    other = 4 - mine
    peers = [lax.rem(col + k, 8) for k in range(1, 8)]
    sources = [lax.rem(col + 8 - k, 8) for k in range(1, 8)]
    xs = [y * 4 + lax.rem(x + k, 4) for k in range(1, 4)]
    ys = [lax.rem(y + k, 4) * 4 + x for k in range(1, 4)]
    place = y * 4 + x
    mate = (1 - zl) * 16 + place

    barrier = pltpu.get_barrier_semaphore()

    def greet(to_row, to_col):
        pl.semaphore_signal(barrier, inc=1, device_id={"row": to_row, "col": to_col}, device_id_type=MESH)

    here = pl.ds(pl.multiple_of(place * 32 + zl * 16, 16), 16)

    def cot_place(c):
        return cots_ref.at[c // 4, here, pl.ds(pl.multiple_of(lax.rem(c, 4) * 128, 128), 128)]

    loads = [
        pltpu.make_async_copy(feat_hbm.at[pl.ds(4 * i, 4)], feat_ref.at[pl.ds(4 * i, 4)], local_sems.at[i])
        for i in range(4)
    ]
    loads.append(pltpu.make_async_copy(cot_hbm, cot_place(col), local_sems.at[4]))
    loads.append(pltpu.make_async_copy(win_hbm, win_ref, local_sems.at[5]))
    loads.append(pltpu.make_async_copy(wout_hbm, wout_ref, local_sems.at[6]))
    loads.append(pltpu.make_async_copy(gain_hbm, norm_ref.at[0], local_sems.at[7]))
    loads.append(pltpu.make_async_copy(shift_hbm, norm_ref.at[1], local_sems.at[8]))
    load_proj = pltpu.make_async_copy(proj_hbm, proj_ref, local_sems.at[9])
    load_proj.start()
    for copy in loads[:5]:
        copy.start()

    for peer in peers:
        greet(row, peer)
    for p in xs + ys:
        greet(zl * 16 + p, col)
    firsts = [(1 - core) * a + core * b for a, b in zip(xs, ys)]
    for p in firsts:
        greet((1 - zl) * 16 + p, col)
    greet(mate, col)
    for k in (1, 3, 5):
        greet(mate, peers[k])

    batch = rows_of(64, 512) & 15
    batch_d = rows_of(64, 128) & 15
    pick = (rows_of(64, 4) >> 4 == lax.broadcasted_iota(jnp.int32, (64, 4), 1)).astype(F32).astype(BF16)
    load_proj.wait()
    proj = mm(pick, proj_ref[...])
    r = rows_of(512, 512)
    perm_ref[...] = (
        (lax.broadcasted_iota(jnp.int32, (512, 512), 1) == (r & 127) * 4 + (r >> 7)).astype(F32).astype(BF16)
    )

    def pair(q):
        return jnp.concatenate([feat_ref[2 * q], feat_ref[2 * q + 1]], axis=1)

    def by_features(left):
        total = jnp.zeros((64, 256), F32)
        for q in range(8):
            total = total + mm(jnp.where(batch >> 1 == q, left, 0.0).astype(BF16), pair(q))
        return jnp.where(batch_d & 1 == 0, total[:, :128], total[:, 128:])

    def spread(value, q):
        return jnp.concatenate(
            [jnp.where(batch_d == 2 * q + i, value, 0.0) for i in range(2)], axis=1
        ).astype(BF16)

    for copy in loads[:4]:
        copy.wait()
    for copy in loads[5:]:
        copy.start()
    reduced = by_features(proj).astype(BF16).astype(F32)
    inter = jnp.zeros((64, 512), F32)
    for q in range(8):
        inter = inter + mm(spread(reduced, q), pair(q), NT)
    blocks = [inter[16 * (j // 2) : 16 * (j // 2) + 16, 256 * (j % 2) : 256 * (j % 2) + 256] for j in range(8)]
    total = blocks[0]
    for j in range(1, 8):
        total = total + blocks[j]
    mean = jnp.sum(total, axis=1, keepdims=True) * (1.0 / 2048)
    for j in range(8):
        part_ref[j] = blocks[j] - mean

    pl.semaphore_wait(barrier, 20)
    links = Links(send_sems, recv_sems)
    where = (x, y, zl, core, row, col)
    gather_n = Gather(links, rows_ref, where)
    gather_c = Gather(links, cots_ref, where)

    def fold(parts, landing, sending, landed):
        copy = links.start(parts.at[pl.ds(other, 4)], landing, landing, row, sibling)
        yield
        copy.wait_recv()
        for j in range(4):
            sending[j] = (parts[mine + j] + landing[j]).astype(BF16)
        copies = [links.start(sending, landed.at[k], landed.at[k], row, peers[2 * k + 1]) for k in (1, 0, 2)]
        yield
        for copy in copies:
            copy.wait_recv()

    fold_inter = fold(part_ref, half_ref, send_ref, got_ref)
    next(fold_inter)
    next(fold_inter)
    loads[4].wait()
    slices = [
        links.start(cot_place(col), cot_place(col), cot_place(source), row, peer)
        for peer, source in zip(peers, sources)
    ]

    loads[5].wait()
    for J in range(4):
        moved = mm(perm_ref[...], win_ref[512 * J : 512 * J + 512, :]).astype(BF16)
        for k in range(4):
            wink_ref[k * 512 + J * 128 : k * 512 + J * 128 + 128, :] = moved[k * 128 : k * 128 + 128, :]
    loads[7].wait()
    loads[8].wait()
    lines = jnp.concatenate([norm_ref[0], norm_ref[1]], axis=0)
    take = (rows_of(8, 32) & 3) * 4 + (rows_of(8, 32) >> 2) * 16
    both = jnp.concatenate(
        [
            mm((lax.broadcasted_iota(jnp.int32, (8, 32), 1) == take + i).astype(F32).astype(BF16), lines)
            for i in range(4)
        ],
        axis=1,
    ).astype(BF16)
    moved = mm(both, perm_ref[...], NT)
    gains = []
    shifts = []
    for j in range(8):
        k, h = j // 2, j % 2
        for base, into in ((0, gains), (4, shifts)):
            J = base + 2 * h
            into.append(
                jnp.concatenate([moved[J + i : J + i + 1, 128 * k : 128 * k + 128] for i in range(2)], axis=1)
            )

    for copy in slices:
        copy.wait_recv()
    gather_c.start_first()
    loads[6].wait()
    dact = jnp.zeros((16, 512), F32)
    for half in range(2):
        dact = dact + mm(cots_ref[half, here, :], wout_ref[:, half * 512 : (half + 1) * 512], NT)

    next(fold_inter, None)
    for j in range(4):
        inter_ref[mine + j] = (send_ref[j].astype(F32) + got_ref[0, j].astype(F32)) + (
            got_ref[1, j].astype(F32) + got_ref[2, j].astype(F32)
        )
    half = inter_ref.at[pl.ds(mine, 4)]
    copy = links.start(half, half, inter_ref.at[pl.ds(other, 4)], row, sibling)
    copy.wait_recv()

    total = inter_ref[0]
    for j in range(1, 8):
        total = total + inter_ref[j]
    mean = jnp.sum(total, axis=1, keepdims=True) * (1.0 / 2048)
    square = jnp.zeros((16, 256), F32)
    for j in range(8):
        centered = inter_ref[j] - mean
        square = square + centered * centered
    rstd = lax.rsqrt(jnp.sum(square, axis=1, keepdims=True) * (1.0 / 2048) + 1e-05)
    normed = []
    for j in range(8):
        unit = (inter_ref[j] - mean) * rstd
        unit_ref[j] = unit
        normed.append((unit * gains[j] + shifts[j]).astype(BF16))
    stacked = jnp.concatenate(
        [
            jnp.concatenate(
                [normed[2 * k + J // 2][:, 128 * (J % 2) : 128 * (J % 2) + 128] for k in range(4)], axis=1
            )
            for J in range(4)
        ],
        axis=0,
    )
    natural = mm(stacked, perm_ref[...]).astype(BF16)
    for J in range(4):
        rows_ref[J // 2, here, 512 * (J % 2) : 512 * (J % 2) + 512] = natural[16 * J : 16 * J + 16, :]
    gather_n.start_first()
    order = (0, 1, -1, 2)

    pre = jnp.zeros((16, 512), F32)
    for j in range(8):
        pre = pre + mm(normed[j], wink_ref[j * 256 : (j + 1) * 256, :])
    sigma = 1.0 / (1.0 + jnp.exp(-pre))
    act = (pre * sigma).astype(BF16)
    dpre = (dact * sigma * (1.0 + pre * (1.0 - sigma))).astype(BF16)
    first = jnp.zeros((16, 256), F32)
    second = jnp.zeros((16, 256), F32)
    gain_terms = []
    shift_terms = []
    scaled = []
    for j in range(8):
        dnormed = mm(dpre, wink_ref[j * 256 : (j + 1) * 256, :], NT)
        gain_terms.append(jnp.sum(dnormed * unit_ref[j], axis=0, keepdims=True))
        shift_terms.append(jnp.sum(dnormed, axis=0, keepdims=True))
        scaled.append(dnormed * gains[j])
        first = first + scaled[j]
        second = second + scaled[j] * unit_ref[j]
    first = jnp.sum(first, axis=1, keepdims=True) * (1.0 / 2048)
    second = jnp.sum(second, axis=1, keepdims=True) * (1.0 / 2048)
    for j in range(8):
        dpart_ref[j] = rstd * (scaled[j] - first - unit_ref[j] * second)
    fold_dinter = fold(dpart_ref, dhalf_ref, dsend_ref, dgot_ref)
    next(fold_dinter)
    for df in order:
        gather_c.start_second(df)
    for h in range(2):
        terms_ref[h] = jnp.concatenate(gain_terms[4 * h : 4 * h + 4] + shift_terms[4 * h : 4 * h + 4], axis=0)
    term = links.start(terms_ref.at[1 - core], term_half_ref, term_half_ref, row, sibling)
    next(fold_dinter)

    def z_of(r, c):
        return (c // 2) * 2 + r // 16

    term.wait_recv()
    at = z_of(row, col)
    term_z_ref[at] = terms_ref[core] + term_half_ref[...]
    terms = []
    for k in range(4):
        for r in (row, mate):
            if k or r is mate:
                to = lax.rem(col + 2 * k, 8)
                source = lax.rem(col + 8 - 2 * k, 8)
                terms.append(
                    links.start(term_z_ref.at[at], term_z_ref.at[at], term_z_ref.at[z_of(r, source)], r, to)
                )
    for j in range(8):
        out_ref[j] = mm(act, wout_ref[:, j * 128 : (j + 1) * 128])
    for df in order:
        gather_n.start_second(df)
    for term in terms:
        term.wait_recv()
    total = term_z_ref[0]
    for k in range(1, 8):
        total = total + term_z_ref[k]
    term_x_ref[x] = total
    terms = [
        links.start(term_x_ref.at[x], term_x_ref.at[x], term_x_ref.at[lax.rem(x + 4 - k, 4)], zl * 16 + xs[k - 1], col)
        for k in range(1, 4)
    ]
    outs = [
        links.start(out_ref.at[peer], got_out_ref.at[k], got_out_ref.at[k], row, peer)
        for k, peer in enumerate(peers)
    ]
    for df in order:
        gather_c.end_second(df)

    next(fold_dinter, None)
    for j in range(4):
        dinter_ref[mine + j] = (
            (dsend_ref[j].astype(F32) + dgot_ref[0, j].astype(F32))
            + (dgot_ref[1, j].astype(F32) + dgot_ref[2, j].astype(F32))
        ).astype(BF16)
    half = dinter_ref.at[pl.ds(mine, 4)]
    copy = links.start(half, half, dinter_ref.at[pl.ds(other, 4)], row, sibling)
    def dacts(i, carry):
        at = pl.ds(pl.multiple_of(i * 256, 256), 256)
        dact_ref[at, :] = mm(cots_ref[0, at, :], wout_ref[:, :512], NT) + mm(
            cots_ref[1, at, :], wout_ref[:, 512:], NT
        )
        return carry

    gather_c.end()
    lax.fori_loop(0, 2, dacts, 0)
    copy.wait_recv()
    dinter = jnp.concatenate(
        [jnp.concatenate([dinter_ref[2 * k], dinter_ref[2 * k + 1]], axis=1) for k in range(4)], axis=0
    ).astype(F32)
    links.flush()
    dreduced = by_features(dinter)
    stores = []
    left = jnp.transpose(jnp.concatenate([dinter, proj], axis=0)).astype(BF16)
    for q in range(8):
        if q == 2:
            for term in terms:
                term.wait_recv()
            term_y_ref[y] = (term_x_ref[0] + term_x_ref[1]) + (term_x_ref[2] + term_x_ref[3])
            terms = [
                links.start(term_y_ref.at[y], term_y_ref.at[y], term_y_ref.at[lax.rem(y + 4 - k, 4)], zl * 16 + ys[k - 1], col)
                for k in range(1, 4)
            ]
        right = jnp.concatenate([spread(reduced, q), spread(dreduced, q)], axis=0)
        grad = mm(left, right).astype(BF16)
        gfeat_ref[2 * q] = grad[:, :128]
        gfeat_ref[2 * q + 1] = grad[:, 128:]
        if q % 2:
            part = pl.ds(2 * q - 2, 4)
            stores.append(
                pltpu.make_async_copy(gfeat_ref.at[part], gfeat_hbm.at[part], store_sems.at[8 + q // 2])
            )
            stores[-1].start()
            gather_n.end_second(order[q // 2])

    mixed = out_ref[col]
    for k, copy in enumerate(outs):
        copy.wait_recv()
        mixed = mixed + got_out_ref[k]
    mixed_ref[...] = mixed.astype(BF16)
    stores.append(pltpu.make_async_copy(mixed_ref, mixed_hbm, store_sems.at[14]))
    stores[-1].start()

    gather_n.end()


    def hidden(i, carry):
        at = pl.ds(pl.multiple_of(i * 256, 256), 256)
        pre = mm(rows_ref[0, at, :], win_ref[:1024, :]) + mm(rows_ref[1, at, :], win_ref[1024:, :])
        sigma = 1.0 / (1.0 + jnp.exp(-pre))
        act_ref[at, :] = (pre * sigma).astype(BF16)
        dpre_ref[at, :] = (dact_ref[at, :] * sigma * (1.0 + pre * (1.0 - sigma))).astype(BF16)
        return carry

    lax.fori_loop(0, 2, hidden, 0)
    for term in terms:
        term.wait_recv()
    term_all_ref[core] = (term_y_ref[0] + term_y_ref[1]) + (term_y_ref[2] + term_y_ref[3])
    term = links.start(term_all_ref.at[core], term_all_ref.at[core], term_all_ref.at[1 - core], row, sibling)

    def grads_in(i, carry):
        at = pl.ds(pl.multiple_of(i * 256, 256), 256)
        columns = pl.ds(pl.multiple_of(lax.rem(i, 4) * 256, 256), 256)
        gwin_ref[at, :] = mm(rows_ref[i // 4, :, columns], dpre_ref[...], TN).astype(BF16)
        pltpu.make_async_copy(gwin_ref.at[at, :], gwin_hbm.at[at, :], store_sems.at[i]).start()
        return carry

    lax.fori_loop(0, 8, grads_in, 0)
    for i in range(8):
        at = pl.ds(i * 256, 256)
        stores.append(pltpu.make_async_copy(gwin_ref.at[at, :], gwin_hbm.at[at, :], store_sems.at[i]))

    term.wait_recv()
    lines = []
    for J in range(4):
        for base in (0, 4):
            lines.append(
                jnp.concatenate(
                    [
                        term_all_ref[
                            k // 2,
                            base + 2 * (k % 2) + J // 2 : base + 2 * (k % 2) + J // 2 + 1,
                            128 * (J % 2) : 128 * (J % 2) + 128,
                        ]
                        for k in range(4)
                    ],
                    axis=1,
                )
            )
    rest = jnp.concatenate(lines, axis=0)
    total = jnp.zeros((8, 512), F32)
    for _ in range(3):
        piece = rest.astype(BF16)
        rest = rest - piece.astype(F32)
        total = total + mm(piece, perm_ref[...])
    for J in range(4):
        gain_out_ref[:, J * 512 : J * 512 + 512] = total[2 * J : 2 * J + 1, :]
        shift_out_ref[:, J * 512 : J * 512 + 512] = total[2 * J + 1 : 2 * J + 2, :]
    stores.append(pltpu.make_async_copy(gain_out_ref, gain_out_hbm, store_sems.at[15]))
    stores[-1].start()
    stores.append(pltpu.make_async_copy(shift_out_ref, shift_out_hbm, store_sems.at[16]))
    stores[-1].start()
    for half in range(2):
        columns = slice(half * 512, (half + 1) * 512)
        gwout_ref[:, columns] = mm(act_ref[...], cots_ref[half], TN).astype(BF16)
        stores.append(
            pltpu.make_async_copy(gwout_ref.at[:, columns], gwout_hbm.at[:, columns], store_sems.at[12 + half])
        )
        stores[-1].start()
    links.flush()
    for copy in stores:
        copy.wait()


def store(*refs):
    loads = [pltpu.make_async_copy(refs[i], refs[12 + i], refs[18].at[i]) for i in (1, 4, 5, 0, 2, 3)]
    saves = [pltpu.make_async_copy(refs[12 + i], refs[6 + i], refs[19].at[i]) for i in (1, 4, 5, 0, 2, 3)]
    for copy in loads:
        copy.start()
    for load, save in zip(loads, saves):
        load.wait()
        save.start()
    for save in saves:
        save.wait()


def on_device(features, projection, norm_gain, norm_shift, weight_in, weight_out, cotangent):
    copies = 130
    hbm = pl.BlockSpec(memory_space=pltpu.HBM)
    results = pl.pallas_call(
        step,
        out_shape=(
            jax.ShapeDtypeStruct((16, 128), BF16),
            jax.ShapeDtypeStruct((16, 512, 128), BF16),
            jax.ShapeDtypeStruct((1, 2048), F32),
            jax.ShapeDtypeStruct((1, 2048), F32),
            jax.ShapeDtypeStruct((2048, 512), BF16),
            jax.ShapeDtypeStruct((512, 1024), BF16),
        ),
        in_specs=[hbm] * 7,
        out_specs=(hbm,) * 6,
        scratch_shapes=[
            pltpu.VMEM((16, 512, 128), BF16),
            pltpu.VMEM((4, 512), BF16),
            pltpu.VMEM((2, 16, 128), BF16),
            pltpu.VMEM((2048, 512), BF16),
            pltpu.VMEM((512, 1024), BF16),
            pltpu.VMEM((2048, 512), BF16),
            pltpu.VMEM((2, 512, 1024), BF16),
            pltpu.VMEM((2, 512, 512), BF16),
            pltpu.VMEM((512, 512), BF16),
            pltpu.VMEM((8, 16, 256), F32),
            pltpu.VMEM((4, 16, 256), F32),
            pltpu.VMEM((4, 16, 256), BF16),
            pltpu.VMEM((3, 4, 16, 256), BF16),
            pltpu.VMEM((8, 16, 256), F32),
            pltpu.VMEM((8, 16, 256), F32),
            pltpu.VMEM((8, 16, 256), F32),
            pltpu.VMEM((4, 16, 256), F32),
            pltpu.VMEM((4, 16, 256), BF16),
            pltpu.VMEM((3, 4, 16, 256), BF16),
            pltpu.VMEM((8, 16, 256), BF16),
            pltpu.VMEM((8, 16, 128), F32),
            pltpu.VMEM((7, 16, 128), F32),
            pltpu.VMEM((2, 8, 256), F32),
            pltpu.VMEM((8, 256), F32),
            pltpu.VMEM((8, 8, 256), F32),
            pltpu.VMEM((4, 8, 256), F32),
            pltpu.VMEM((4, 8, 256), F32),
            pltpu.VMEM((2, 8, 256), F32),
            pltpu.VMEM((512, 512), BF16),
            pltpu.VMEM((512, 512), BF16),
            pltpu.VMEM((512, 512), F32),
            pltpu.VMEM((16, 512, 128), BF16),
            pltpu.VMEM((2048, 512), BF16),
            pltpu.VMEM((512, 1024), BF16),
            pltpu.VMEM((16, 128), BF16),
            pltpu.VMEM((1, 2048), F32),
            pltpu.VMEM((1, 2048), F32),
            pltpu.SemaphoreType.DMA((copies,)),
            pltpu.SemaphoreType.DMA((copies,)),
            pltpu.SemaphoreType.DMA((10,)),
            pltpu.SemaphoreType.DMA((17,)),
        ],
        compiler_params=pltpu.CompilerParams(
            collective_id=0, has_side_effects=True, vmem_limit_bytes=58 * 1024 * 1024
        ),
    )(
        features,
        projection.T,
        norm_gain.reshape(16, 128),
        norm_shift.reshape(16, 128),
        weight_in,
        weight_out.reshape(weight_out.shape[0], -1),
        cotangent.reshape(cotangent.shape[0], -1),
    )
    mixed, gfeat, gain, shift, gwin, gwout = pl.pallas_call(
        store,
        out_shape=tuple(jax.ShapeDtypeStruct(a.shape, a.dtype) for a in results),
        in_specs=[pl.BlockSpec(memory_space=pl.ANY)] * 6,
        out_specs=(hbm,) * 6,
        scratch_shapes=[pltpu.VMEM(a.shape, a.dtype) for a in results]
        + [pltpu.SemaphoreType.DMA((6,)), pltpu.SemaphoreType.DMA((6,))],
        compiler_params=pltpu.CompilerParams(vmem_limit_bytes=58 * 1024 * 1024),
    )(*results)
    return (
        mixed.reshape(cotangent.shape),
        gfeat,
        gain.reshape(-1),
        shift.reshape(-1),
        gwin,
        gwout.reshape(weight_out.shape),
    )


def solution(mesh):
    placed = (
        P("row", None, "col"),
        P(),
        P(),
        P(),
        P(None, "col"),
        P("col", None, None),
        P("row", None, "col"),
    )
    return jax.shard_map(
        on_device,
        mesh=mesh,
        in_specs=placed,
        out_specs=(
            P("row", None, "col"),
            P("row", None, "col"),
            P(),
            P(),
            P(None, "col"),
            P("col", None, None),
        ),
        check_vma=False,
    )
```
